32 devices in a mesh: ha: 4 (over y, x), wa: 8 (over z, core).
Axes of the slice: x: 2, y: 2, z: 4, core: 2. Of those that a mesh axis runs over, the one named last changes fastest.
Arguments:
- velocity: float32 [2, 256, 1024], P(None, 'wa', 'ha'), may hold values from -6 to 6
- cotangent: float32 [2, 256, 1024], P(None, 'wa', 'ha'), may hold values from -6 to 6
- lift_weight: float32 [64, 2], replicated, may hold values from -4 to 4
- depth_kernels: float32 [1, 64, 9], replicated, may hold values from -2 to 2
- point_weights: bfloat16 [1, 64, 64], replicated, may hold values from -0.75 to 0.75
- out_weight: bfloat16 [2, 64], replicated, may hold values from -0.75 to 0.75
Outputs:
- grad_velocity: float32 [2, 256, 1024], P(None, 'wa', 'ha')
- grad_lift: float32 [64, 2], replicated
- grad_kernels: float32 [1, 64, 9], replicated
- grad_point: float32 [1, 64, 64], replicated
- grad_out: float32 [2, 64], replicated
The draws below stay inside these ranges and needn't reach their ends.
All inputs are finite; a program needn't handle non-finite values.
Results may differ from the reference program's by a relative error of at most 0.012.
Values may be sent and summed in bfloat16 or wider, within the bound.
A program may use at most 64 MiB of HBM per device.

```python
import math
import jax
import jax.numpy as jnp
from jax import lax

C = 64
LAYERS = 1
CW = 32
NX = 256
NY = 1024


def steps_of(own_key, extent, split, smallest, high):
    def one(position, shards_of):
        draws = jax.random.uniform(jax.random.fold_in(jax.random.fold_in(own_key, 6), position), (shards_of,), jnp.float32, smallest / len(split), high / len(split))
        return jnp.repeat(jnp.exp(draws), extent[position] // shards_of).reshape((-1,) + (1,) * (len(extent) - position - 1))

    level = one(*split[0])
    for cut in split[1:]:
        level = level * one(*cut)
    return level


def gaussian(own_key, dims, scale, reach, split=(), kind=jnp.bfloat16):
    loudness = steps_of(own_key, dims, split, -0.22, 0.18) if split else 1.0
    values = jax.random.normal(own_key, dims, jnp.float32) * scale * loudness
    return jnp.minimum(jnp.maximum(values, -reach), reach).astype(kind)


def setup_inputs(seed: int = 0) -> dict:
    splits = jax.random.split(jax.random.key(seed), 7)
    velocity = gaussian(splits[0], (2, NX, NY), 1.0, 6.0, ((1, 8), (2, 4)), jnp.float32)
    cotangent = gaussian(splits[1], (2, NX, NY), 1.0, 6.0, ((1, 8), (2, 4)), jnp.float32)
    lift_weight = gaussian(splits[2], (C, 2), 2 ** -0.5, 4.0, (), jnp.float32)
    depth_kernels = gaussian(splits[3], (LAYERS, C, 9), 9 ** -0.5, 2.0, (), jnp.float32)
    point_weights = gaussian(splits[4], (LAYERS, C, C), C ** -0.5, 0.75)
    out_weight = gaussian(splits[5], (2, C), C ** -0.5, 0.75)
    return dict(velocity=velocity, cotangent=cotangent, lift_weight=lift_weight, depth_kernels=depth_kernels, point_weights=point_weights, out_weight=out_weight)


OFFSETS = ((-1, -1), (-1, 0), (-1, 1), (0, -1), (0, 0), (0, 1), (1, -1), (1, 0), (1, 1))

def signed_waves(count_n):
    ids = jnp.arange(count_n, dtype=jnp.int32)
    return jnp.where(2 * ids >= count_n, ids - count_n, ids).astype(jnp.float32)

def shifted(values, step_x, step_y):
    return jnp.roll(values, (-step_x, -step_y), axis=(1, 2))

def reference(velocity, cotangent, lift_weight, depth_kernels, point_weights, out_weight):
    highest = lax.Precision.HIGHEST
    spectrum = jnp.fft.fft2(cotangent, axes=(1, 2))
    wave_x = signed_waves(NX)[:, None]
    wave_y = signed_waves(NY)[None, :]
    along_k = wave_x * spectrum[0] + wave_y * spectrum[1]
    factor = along_k / jnp.maximum(wave_x * wave_x + wave_y * wave_y, 1.0)
    projected = jnp.stack([spectrum[0] - wave_x * factor, spectrum[1] - wave_y * factor])
    grad_proj = jnp.real(jnp.fft.ifft2(projected, axes=(1, 2))).astype(jnp.float32)
    margin = 2 * LAYERS
    extent_rows = CW + 2 * margin
    point_full = point_weights.astype(jnp.float32)
    out_full = out_weight.astype(jnp.float32)

    def band(totals, band_index):
        row_ids = (band_index * CW - margin + jnp.arange(extent_rows, dtype=jnp.int32)) % NX
        field_band = jnp.take(velocity, row_ids, axis=1)
        grad_band = jnp.take(grad_proj, row_ids, axis=1)
        hidden = jnp.einsum('cs,sxy->cxy', lift_weight, field_band, precision=highest).astype(jnp.bfloat16)
        saved_in, saved_depth, saved_tanh = ([], [], [])
        for layer_id in range(LAYERS):
            depth_acc = jnp.zeros(hidden.shape, jnp.float32)
            for offset_id in range(9):
                step_x, step_y = OFFSETS[offset_id]
                depth_acc = depth_acc + depth_kernels[layer_id, :, offset_id][:, None, None] * shifted(hidden, step_x, step_y).astype(jnp.float32)
            depth_out = depth_acc.astype(jnp.bfloat16)
            mixed_pre = jnp.einsum('oc,cxy->oxy', point_full[layer_id], depth_out.astype(jnp.float32), precision=highest)
            squash = jnp.tanh(mixed_pre).astype(jnp.bfloat16)
            saved_in.append(hidden)
            saved_depth.append(depth_out)
            saved_tanh.append(squash)
            hidden = (hidden.astype(jnp.float32) + squash.astype(jnp.float32)).astype(jnp.bfloat16)
        grad_b = grad_band.astype(jnp.bfloat16).astype(jnp.float32)
        lo_row = margin
        hi_row = margin + CW
        out_sum = jnp.einsum('sxy,cxy->sc', grad_b[:, lo_row:hi_row], hidden[:, lo_row:hi_row].astype(jnp.float32), precision=highest)
        grad_hidden = jnp.einsum('sc,sxy->cxy', out_full, grad_b, precision=highest)
        kernel_sums = [None] * LAYERS
        point_sums = [None] * LAYERS
        for layer_id in reversed(range(LAYERS)):
            squash_full = saved_tanh[layer_id].astype(jnp.float32)
            grad_mixed = (grad_hidden * (1.0 - squash_full * squash_full)).astype(jnp.bfloat16).astype(jnp.float32)
            point_sums[layer_id] = jnp.einsum('oxy,cxy->oc', grad_mixed[:, lo_row:hi_row], saved_depth[layer_id][:, lo_row:hi_row].astype(jnp.float32), precision=highest)
            grad_depth = jnp.einsum('oc,oxy->cxy', point_full[layer_id], grad_mixed, precision=highest).astype(jnp.bfloat16).astype(jnp.float32)
            entries = []
            for offset_id in range(9):
                step_x, step_y = OFFSETS[offset_id]
                moved_in = shifted(saved_in[layer_id], step_x, step_y).astype(jnp.float32)
                entries.append(lax.optimization_barrier(jnp.sum(grad_depth[:, lo_row:hi_row] * moved_in[:, lo_row:hi_row], axis=(1, 2))))
                grad_hidden = grad_hidden + depth_kernels[layer_id, :, offset_id][:, None, None] * jnp.roll(grad_depth, (step_x, step_y), axis=(1, 2))
            kernel_sums[layer_id] = jnp.stack(entries, axis=1)
        lift_sum = jnp.einsum('cxy,sxy->cs', grad_hidden[:, lo_row:hi_row], field_band[:, lo_row:hi_row], precision=highest)
        grad_rows = grad_band[:, lo_row:hi_row] + jnp.einsum('cs,cxy->sxy', lift_weight, grad_hidden[:, lo_row:hi_row], precision=highest)
        new_totals = (totals[0] + lift_sum, totals[1] + jnp.stack(kernel_sums), totals[2] + jnp.stack(point_sums), totals[3] + out_sum)
        return (new_totals, grad_rows)
    start = (jnp.zeros((C, 2), jnp.float32), jnp.zeros((LAYERS, C, 9), jnp.float32), jnp.zeros((LAYERS, C, C), jnp.float32), jnp.zeros((2, C), jnp.float32))
    totals, bands = lax.scan(band, start, jnp.arange(NX // CW, dtype=jnp.int32))
    grad_velocity = jnp.transpose(bands, (1, 0, 2, 3)).reshape(2, NX, NY)
    scale = 1.0 / math.sqrt(NX * NY)
    return (grad_velocity, totals[0] * scale, totals[1] * scale, totals[2] * scale, totals[3] * scale)
```

```python
import functools
import math

import jax
import jax.numpy as jnp
import ml_dtypes
import numpy as np
from jax import lax
from jax.experimental import pallas as pl
from jax.experimental.pallas import tpu as pltpu
from jax.sharding import PartitionSpec as P

OFFSETS = ((-1, -1), (-1, 0), (-1, 1), (0, -1), (0, 0), (0, 1), (1, -1), (1, 0), (1, 1))
TWO_PI = 2.0 * math.pi


def extended(value, sides, width):
    for axis, dim in sides:
        size, length = (lax.axis_size(axis), value.shape[dim])
        up = [(i, (i + 1) % size) for i in range(size)]
        down = [(j, i) for i, j in up]
        last = lax.slice_in_dim(value, length - width, length, axis=dim)
        leading = lax.slice_in_dim(value, 0, width, axis=dim)
        before = lax.ppermute(last, axis, up)
        after = lax.ppermute(leading, axis, down)
        value = jnp.concatenate([before, value, after], axis=dim)
    return value


def dft_table(table_len, sign_val):
    ids = jnp.arange(table_len, dtype=jnp.int32)
    product = ids[:, None] * ids[None, :] % table_len
    phase_angle = sign_val * TWO_PI / table_len * product.astype(jnp.float32)
    return (jnp.cos(phase_angle), jnp.sin(phase_angle))


def apply_table(values, tab_real, tab_imag):
    highest = lax.Precision.HIGHEST
    real_part = values[0]
    imag_part = values[1]
    out_real = jnp.einsum("...n,kn->...k", real_part, tab_real, precision=highest) - jnp.einsum(
        "...n,kn->...k", imag_part, tab_imag, precision=highest
    )
    out_imag = jnp.einsum("...n,kn->...k", real_part, tab_imag, precision=highest) + jnp.einsum(
        "...n,kn->...k", imag_part, tab_real, precision=highest
    )
    return jnp.stack([out_real, out_imag])


def rotate(values, phase_angle):
    cosine = jnp.cos(phase_angle)
    sine_val = jnp.sin(phase_angle)
    return jnp.stack(
        [values[0] * cosine - values[1] * sine_val, values[0] * sine_val + values[1] * cosine]
    )


def forward_first(values, axis_dim, groups, own_index, length):
    moved = jnp.moveaxis(values, axis_dim, -1)
    leading = moved.shape[:-1]
    full_len = moved.shape[-1]
    piece_len = full_len // groups
    moved = jnp.swapaxes(moved.reshape(leading + (groups, piece_len)), -1, -2)
    tab_real, tab_imag = dft_table(groups, -1.0)
    moved = apply_table(moved, tab_real, tab_imag)
    local_m = jnp.arange(piece_len, dtype=jnp.int32)[:, None] + own_index * piece_len
    first_k = jnp.arange(groups, dtype=jnp.int32)[None, :]
    phase_angle = -TWO_PI / length * (local_m * first_k % length).astype(jnp.float32)
    moved = rotate(moved, phase_angle)
    moved = jnp.swapaxes(moved, -1, -2).reshape(leading + (full_len,))
    return jnp.moveaxis(moved, -1, axis_dim)


def forward_second(values, axis_dim):
    moved = jnp.moveaxis(values, axis_dim, -1)
    tab_real, tab_imag = dft_table(moved.shape[-1], -1.0)
    moved = apply_table(moved, tab_real, tab_imag)
    return jnp.moveaxis(moved, -1, axis_dim)


def inverse_first(values, axis_dim, own_index, length):
    moved = jnp.moveaxis(values, axis_dim, -1)
    full_len = moved.shape[-1]
    tab_real, tab_imag = dft_table(full_len, 1.0)
    moved = apply_table(moved, tab_real, tab_imag)
    local_m = jnp.arange(full_len, dtype=jnp.int32)
    phase_angle = TWO_PI / length * (local_m * own_index % length).astype(jnp.float32)
    moved = rotate(moved, phase_angle)
    return jnp.moveaxis(moved, -1, axis_dim)


def inverse_second(values, axis_dim, groups):
    moved = jnp.moveaxis(values, axis_dim, -1)
    leading = moved.shape[:-1]
    full_len = moved.shape[-1]
    piece_len = full_len // groups
    moved = jnp.swapaxes(moved.reshape(leading + (groups, piece_len)), -1, -2)
    tab_real, tab_imag = dft_table(groups, 1.0)
    moved = apply_table(moved, tab_real, tab_imag)
    moved = jnp.swapaxes(moved, -1, -2).reshape(leading + (full_len,))
    return jnp.moveaxis(moved, -1, axis_dim)


def signed_waves(own_index, groups, count_n):
    ids = own_index + groups * jnp.arange(count_n, dtype=jnp.int32)
    total_len = groups * count_n
    return jnp.where(2 * ids >= total_len, ids - total_len, ids).astype(jnp.float32)


def project(spectrum, wave_x, wave_y):
    along_k = wave_x * spectrum[:, 0] + wave_y * spectrum[:, 1]
    factor = along_k / jnp.maximum(wave_x * wave_x + wave_y * wave_y, 1.0)
    return jnp.stack([spectrum[:, 0] - wave_x * factor, spectrum[:, 1] - wave_y * factor], axis=1)


def depthwise_valid(padded, kernel):
    rows_in = padded.shape[1] - 2
    cols_in = padded.shape[2] - 2
    total = jnp.zeros((padded.shape[0], rows_in, cols_in), jnp.float32)
    for offset_id in range(9):
        step_x, step_y = OFFSETS[offset_id]
        total = (
            total
            + kernel[:, offset_id][:, None, None]
            * padded[:, 1 + step_x : 1 + step_x + rows_in, 1 + step_y : 1 + step_y + cols_in]
        )
    return total


def transposed_add(grad_hidden, grad_pad, kernel):
    rows_in = grad_hidden.shape[1]
    cols_in = grad_hidden.shape[2]
    for offset_id in range(9):
        step_x, step_y = OFFSETS[offset_id]
        grad_hidden = (
            grad_hidden
            + kernel[:, offset_id][:, None, None]
            * grad_pad[:, 1 - step_x : 1 - step_x + rows_in, 1 - step_y : 1 - step_y + cols_in]
        )
    return grad_hidden


def kernel_grad(grad_depth, padded):
    rows_in = grad_depth.shape[1]
    cols_in = grad_depth.shape[2]
    grad_full = grad_depth.astype(jnp.float32)
    entries = []
    for offset_id in range(9):
        step_x, step_y = OFFSETS[offset_id]
        window = padded[
            :, 1 + step_x : 1 + step_x + rows_in, 1 + step_y : 1 + step_y + cols_in
        ].astype(jnp.float32)
        entries.append(jnp.sum(grad_full * window, axis=(1, 2)))
    return jnp.stack(entries, axis=1)


def local(velocity, cotangent, lift_weight, depth_kernels, point_weights, out_weight):
    highest = lax.Precision.HIGHEST
    layers = depth_kernels.shape[0]
    cols_n = velocity.shape[1]
    rows_n = velocity.shape[2]
    groups_x = lax.axis_size("wa")
    groups_y = lax.axis_size("ha")
    own_x = lax.axis_index("wa")
    own_y = lax.axis_index("ha")
    length_x = cols_n * groups_x
    length_y = rows_n * groups_y
    spectrum = jnp.stack([cotangent, jnp.zeros_like(cotangent)])
    wave_x = signed_waves(own_x, groups_x, cols_n)[:, None]
    wave_y = signed_waves(own_y, groups_y, rows_n)[None, :]

    def move_x(values):
        return lax.all_to_all(values, "wa", split_axis=2, concat_axis=2, tiled=True)

    def move_y(values):
        return lax.all_to_all(values, "ha", split_axis=3, concat_axis=3, tiled=True)

    spectrum = forward_first(move_x(spectrum), 2, groups_x, own_x, length_x)
    spectrum = forward_second(move_x(spectrum), 2)
    spectrum = forward_first(move_y(spectrum), 3, groups_y, own_y, length_y)
    spectrum = forward_second(move_y(spectrum), 3)
    spectrum = project(spectrum, wave_x, wave_y)
    spectrum = move_y(inverse_first(spectrum, 3, own_y, length_y))
    spectrum = move_y(inverse_second(spectrum, 3, groups_y))
    spectrum = move_x(inverse_first(spectrum, 2, own_x, length_x))
    spectrum = move_x(inverse_second(spectrum, 2, groups_x))
    grad_proj = spectrum[0] / float(length_x * length_y)
    saved_pad, saved_depth, saved_tanh = ([], [], [])
    hidden = jnp.einsum("cs,sxy->cxy", lift_weight, velocity, precision=highest).astype(
        jnp.bfloat16
    )
    layer_id = 0
    padded = extended(hidden, (("ha", 2), ("wa", 1)), 1)
    depth_out = depthwise_valid(padded, depth_kernels[layer_id]).astype(jnp.bfloat16)
    mixed_pre = jnp.einsum(
        "oc,cxy->oxy", point_weights[layer_id], depth_out, preferred_element_type=jnp.float32
    )
    squash = jnp.tanh(mixed_pre).astype(jnp.bfloat16)
    saved_pad.append(padded)
    saved_depth.append(depth_out)
    saved_tanh.append(squash)
    hidden = (hidden.astype(jnp.float32) + squash.astype(jnp.float32)).astype(jnp.bfloat16)
    grad_proj_b = grad_proj.astype(jnp.bfloat16)
    out_sum = jnp.einsum("sxy,cxy->sc", grad_proj_b, hidden, preferred_element_type=jnp.float32)
    grad_hidden = jnp.einsum(
        "sc,sxy->cxy", out_weight, grad_proj_b, preferred_element_type=jnp.float32
    )
    kernel_sums = [None] * layers
    point_sums = [None] * layers
    for layer_id in reversed(range(layers)):
        squash_full = saved_tanh[layer_id].astype(jnp.float32)
        grad_mixed = (grad_hidden * (1.0 - squash_full * squash_full)).astype(jnp.bfloat16)
        point_sums[layer_id] = jnp.einsum(
            "oxy,cxy->oc", grad_mixed, saved_depth[layer_id], preferred_element_type=jnp.float32
        )
        grad_depth = jnp.einsum(
            "oc,oxy->cxy", point_weights[layer_id], grad_mixed, preferred_element_type=jnp.float32
        ).astype(jnp.bfloat16)
        grad_pad = extended(grad_depth, (("ha", 2), ("wa", 1)), 1)
        kernel_sums[layer_id] = kernel_grad(grad_depth, saved_pad[layer_id])
        grad_hidden = transposed_add(grad_hidden, grad_pad, depth_kernels[layer_id])
    lift_sum = jnp.einsum("cxy,sxy->cs", grad_hidden, velocity, precision=highest)
    grad_velocity = grad_proj + jnp.einsum(
        "cs,cxy->sxy", lift_weight, grad_hidden, precision=highest
    )
    totals = lax.psum(
        (lift_sum, jnp.stack(kernel_sums), jnp.stack(point_sums), out_sum), ("ha", "wa")
    )
    scale = 1.0 / math.sqrt(length_x * length_y)
    return (
        grad_velocity,
        totals[0] * scale,
        totals[1] * scale,
        totals[2] * scale,
        totals[3] * scale,
    )


def real_basis(pairs, is_sin, positions, length):
    angle = 2.0 * np.pi / length * (np.outer(pairs, positions) % length)
    sines = np.where(pairs[:, None] == 0, np.cos(np.pi * positions)[None, :], np.sin(angle))
    return np.where(is_sin[:, None], sines, np.cos(angle))


def make_tables(groups_y, groups_x, rows, cols):
    length_x, length_y = groups_x * rows, groups_y * cols
    per = length_y // (groups_x * groups_y)
    half = per // 2
    ids = np.arange(length_y)
    pair_y = (ids // per) * half + ids % half
    sin_y = (ids % per) >= half
    forward_y = real_basis(pair_y, sin_y, np.arange(length_y), length_y)
    forward_y = forward_y.reshape(groups_y, cols, length_y)
    lanes = np.arange(cols + 128)
    local_y = np.where(lanes > cols, -1, lanes)
    keep_y = (lanes <= cols) | (lanes == cols + 127)
    inverse_y = np.stack(
        [
            real_basis(pair_y, sin_y, (h * cols + local_y) % length_y, length_y) * keep_y
            for h in range(groups_y)
        ]
    )
    kx = np.arange(length_x)
    pair_x = kx % (length_x // 2)
    sin_x = kx >= length_x // 2
    basis_x = real_basis(pair_x, sin_x, np.arange(length_x), length_x)
    forward_x = np.zeros((groups_x, 2, rows, 2, length_x))
    band = rows + 8
    inverse_x = np.zeros((2, length_x, groups_x, 128))
    local_x = np.arange(band)
    keep_x = (local_x <= rows) | (local_x == band - 1)
    local_x = np.where(local_x > rows, -1, local_x)
    for s in range(2):
        forward_x[:, s, :, s, :] = basis_x.T.reshape(groups_x, rows, length_x)
        for w in range(groups_x):
            part = basis_x[:, (w * rows + local_x) % length_x] * keep_x
            inverse_x[s, :, w, s * band : (s + 1) * band] = part
    forward_x = forward_x.reshape(groups_x, 2 * rows, 2 * length_x)
    inverse_x = inverse_x.reshape(2 * length_x, groups_x * 128)

    def halves(table, axis):
        coarse = table.astype(ml_dtypes.bfloat16)
        fine = (table - coarse.astype(np.float64)).astype(ml_dtypes.bfloat16)
        return np.stack([coarse, fine], axis=axis)

    forward_x = halves(forward_x, 1)
    forward_x = np.concatenate([forward_x[:, 0], forward_x[:, 0], forward_x[:, 1]], axis=1)
    return halves(forward_y, 1), halves(inverse_y, 1), forward_x, halves(inverse_x, 0)


def selectors():
    lift = np.zeros((2, 24), np.float32)
    taps = np.zeros((9, 24), np.float32)
    for a in range(3):
        for s in range(2):
            for b in range(3):
                lift[s, a * 8 + s * 3 + b] = 1.0
                taps[3 * a + b, a * 8 + s * 3 + b] = 1.0
    middle = np.zeros((32, 2), np.float32)
    middle[9, 0] = 1.0
    middle[12, 1] = 1.0
    return lift, taps, middle


def dot(a, b, dims=((1,), (0,)), exact=False):
    return lax.dot_general(
        a,
        b,
        (dims, ((), ())),
        precision=lax.Precision.HIGHEST if exact else None,
        preferred_element_type=jnp.float32,
    )


def put(ref, start, count, stride, value):
    for tile in range(ref.shape[0]):
        ref[tile, pl.ds(start, count, stride=stride), :] = value[:, tile * 128 : (tile + 1) * 128]


def take(ref, start, count, stride=1, tiles=None):
    rows = pl.ds(start, count, stride=stride)
    parts = [ref[tile, rows, :] for tile in range(tiles or ref.shape[0])]
    return jnp.concatenate(parts, axis=1)


def halved(value, axis):
    coarse = value.astype(jnp.bfloat16)
    fine = (value - coarse.astype(jnp.float32)).astype(jnp.bfloat16)
    return jnp.concatenate([coarse, fine], axis=axis)


def fused_kernel(
    groups_y,
    groups_x,
    rows,
    cols,
    vel_ref,
    cot_ref,
    lift_ref,
    taps_ref,
    point_ref,
    outw_ref,
    sel_lift_ref,
    sel_taps_ref,
    sel_mid_ref,
    fy_hbm,
    iy_hbm,
    fx_hbm,
    ix_hbm,
    gv_ref,
    glift_ref,
    gtaps_ref,
    gpoint_ref,
    gout_ref,
    fy,
    iy,
    fx,
    ix,
    gath,
    send2,
    recv2,
    send3,
    recv3,
    gath4,
    halo_out,
    halo_in,
    edge_out,
    edge_in,
    ext,
    shifts,
    tbuf,
    slope,
    gp2,
    ubuf,
    pay_y,
    pay_x,
    table_sem,
    s1,
    r1,
    s2,
    r2,
    s3,
    r3,
    s4,
    r4,
    sh,
    rh,
    se,
    re,
    s5,
    r5,
    s6,
    r6,
):
    bf16, f32 = jnp.bfloat16, jnp.float32
    h = lax.axis_index("ha")
    w = lax.axis_index("wa")
    length_x, length_y = groups_x * rows, groups_y * cols
    per = length_y // (groups_x * groups_y)
    half = per // 2
    wide = cols + 128
    band = rows + 8

    loads = [
        pltpu.make_async_copy(fy_hbm.at[h], fy, table_sem.at[0]),
        pltpu.make_async_copy(iy_hbm.at[h], iy, table_sem.at[1]),
        pltpu.make_async_copy(fx_hbm, fx, table_sem.at[2]),
        pltpu.make_async_copy(ix_hbm, ix, table_sem.at[3]),
    ]
    for load in (loads[0], loads[2], loads[3], loads[1]):
        load.start()

    def ha_peer(step):
        return lax.rem(h + step, groups_y)

    def wa_peer(step):
        return lax.rem(w + step, groups_x)

    barrier = pltpu.get_barrier_semaphore()
    for step in range(1, groups_y):
        pl.semaphore_signal(
            barrier, inc=1, device_id=(ha_peer(step), w), device_id_type=pl.DeviceIdType.MESH
        )
    for step in range(1, groups_x):
        pl.semaphore_signal(
            barrier, inc=1, device_id=(h, wa_peer(step)), device_id_type=pl.DeviceIdType.MESH
        )

    def remote(src, dst, send, recv, device):
        return pltpu.make_async_remote_copy(
            src_ref=src,
            dst_ref=dst,
            send_sem=send,
            recv_sem=recv,
            device_id=device,
            device_id_type=pl.DeviceIdType.MESH,
        )

    gath[h] = halved(cot_ref[...].reshape(2 * rows, cols), 0)
    vel = vel_ref[...].reshape(2 * rows, cols)
    halo_out[0] = vel[:, :128]
    halo_out[1] = vel[:, cols - 128 :]
    pl.semaphore_wait(barrier, groups_y + groups_x - 2)

    def spread_y(buf, send, recv):
        copies = []
        for step in range(1, groups_y):
            copy = remote(buf.at[h], buf.at[h], send.at[step], recv.at[h], (ha_peer(step), w))
            copy.start()
            copies.append(copy)
        return copies

    def arrived_y(buf, send, recv, step):
        src = ha_peer(step)
        remote(buf.at[src], buf.at[src], send.at[step], recv.at[src], (src, w)).wait_recv()
        return src

    def spread_x(src_of, buf, send, recv):
        copies = []
        for step in range(1, groups_x):
            dst = wa_peer(step)
            copy = remote(src_of(dst), buf.at[w], send.at[step], recv.at[w], (h, dst))
            copy.start()
            copies.append(copy)
        return copies

    def arrived_x(buf, send, recv, step):
        src = wa_peer(step)
        remote(buf.at[src], buf.at[src], send.at[step], recv.at[src], (h, src)).wait_recv()

    pending = spread_y(gath, s1, r1)
    left, right = (ha_peer(groups_y - 1), w), (ha_peer(1), w)
    halo = [
        remote(halo_out.at[0], halo_in.at[0], sh.at[0], rh.at[0], left),
        remote(halo_out.at[1], halo_in.at[1], sh.at[1], rh.at[1], right),
    ]
    for copy in halo:
        copy.start()

    lift_wide = dot(lift_ref[...], sel_lift_ref[...], exact=True)
    taps_wide = dot(taps_ref[0], sel_taps_ref[...], exact=True)
    both = lift_wide * taps_wide
    point = point_ref[0].astype(f32)
    mixed = dot(point, both, exact=True)
    coarse = mixed.astype(bf16).astype(f32)
    mixed_b = jnp.concatenate(
        [coarse, mixed - coarse, coarse, jnp.zeros_like(coarse[:, :8])], axis=1
    ).astype(bf16)
    none = jnp.zeros((8, wide), f32)
    outw = outw_ref[...].astype(f32)
    out_pad = jnp.concatenate([outw, jnp.zeros((14, outw.shape[1]), f32)], axis=0)
    out_b = out_pad.astype(bf16)
    through = dot(lift_ref[...], out_pad, ((0,), (1,)), exact=True)
    place = sel_mid_ref[...][:24]
    back_b = jnp.concatenate(
        [jnp.transpose(jnp.pad(mixed, ((0, 64), (0, 104))))[:24, :64], dot(place, through, exact=True)],
        axis=1,
    ).astype(bf16)

    row_id = lax.broadcasted_iota(jnp.int32, (per, length_x), 0)
    lane_id = lax.broadcasted_iota(jnp.int32, (per, length_x), 1)
    py = (h * groups_x + w) * half + lax.rem(row_id, half)
    px = lax.rem(lane_id, length_x // 2)
    ysin, xsin = row_id >= half, lane_id >= length_x // 2
    ky = jnp.where((py == 0) & ysin, length_y // 2, py).astype(f32)
    kx = jnp.where((px == 0) & xsin, length_x // 2, px).astype(f32)
    weight = jnp.where(py == 0, 1.0, 2.0) * jnp.where(px == 0, 1.0, 2.0) / (length_x * length_y)
    inverse_k = weight / jnp.maximum(kx * kx + ky * ky, 1.0)
    keep_0 = weight - kx * kx * inverse_k
    keep_1 = weight - ky * ky * inverse_k
    cross = kx * ky * inverse_k
    inner = (px != 0) & (py != 0)
    turn = jnp.where(inner, jnp.where(ysin == xsin, -cross, cross), 0.0)
    corner = jnp.where((px == 0) & (py == 0) & ysin & xsin, cross, 0.0)

    loads[0].wait()
    spec = jnp.zeros((cols, 2 * rows), f32)
    for step in range(groups_y):
        src = h if step == 0 else arrived_y(gath, s1, r1, step)
        where = pl.ds(pl.multiple_of(src * cols, cols), cols)
        field = gath[src]
        both_parts = dot(fy[0, :, where], field, ((1,), (1,)))
        spec = spec + both_parts[:, : 2 * rows] + both_parts[:, 2 * rows :]
        spec = spec + dot(fy[1, :, where], field[: 2 * rows], ((1,), (1,)))
    send2[...] = halved(spec, 1).reshape(groups_x, per, 4 * rows)
    pending += spread_x(lambda dst: send2.at[dst], recv2, s2, r2)
    recv2[w] = send2[w]

    for copy in halo:
        copy.wait()
    side = lax.broadcasted_iota(jnp.int32, (2 * rows, 128), 1)
    tail = jnp.where(side < 64, halo_in[0], halo_in[1])
    ext[:, :cols] = vel
    ext[:, cols:] = tail
    edge_out[...] = jnp.zeros_like(edge_out)
    for s in range(2):
        edge_out[0, 2 * s : 2 * s + 2, :] = ext[s * rows : s * rows + 2, :]
        edge_out[1, 2 * s : 2 * s + 2, :] = ext[s * rows + rows - 2 : s * rows + rows, :]
    edges = [
        remote(edge_out.at[0], edge_in.at[0], se.at[0], re.at[0], (h, wa_peer(groups_x - 1))),
        remote(edge_out.at[1], edge_in.at[1], se.at[1], re.at[1], (h, wa_peer(1))),
    ]
    for copy in edges:
        copy.start()
    shifts[...] = jnp.zeros_like(shifts)
    for s in range(2):
        for b in range(3):
            moved = ext[s * rows : (s + 1) * rows, :]
            if b != 1:
                moved = pltpu.roll(moved, (1 - b) % wide, 1)
            put(shifts, 16 + s * 3 + b, rows, 8, moved)

    loads[2].wait()
    for step in range(1, groups_x):
        arrived_x(recv2, s2, r2, step)
    waves = jnp.zeros((per, 2 * length_x), f32)
    for src in range(groups_x):
        got = recv2[src]
        waves = waves + dot(jnp.concatenate([got, got[:, : 2 * rows]], axis=1), fx[src])
    a0, a1 = waves[:, :length_x], waves[:, length_x:]

    def swapped(a):
        a = jnp.concatenate([a[half:], a[:half]], axis=0)
        return jnp.concatenate([a[:, length_x // 2 :], a[:, : length_x // 2]], axis=1)

    p0 = keep_0 * a0 - turn * swapped(a1) - corner * a1
    p1 = keep_1 * a1 - turn * swapped(a0) - corner * a0
    loads[3].wait()
    split = halved(jnp.concatenate([p0, p1], axis=1), 0)
    fields = dot(split, ix[0])
    fields = fields[:per] + fields[per:] + dot(split[:per], ix[1])
    for dst in range(groups_x):
        send3[dst] = fields[:, dst * 128 : (dst + 1) * 128]
    pending += spread_x(lambda dst: send3.at[dst], recv3, s3, r3)
    recv3[w] = send3[w]

    for copy in edges:
        copy.wait()
    for s in range(2):
        for b in range(3):
            for slot, first in ((1, 0), (0, rows + 2)):
                moved = edge_in[slot]
                if b != 1:
                    moved = pltpu.roll(moved, (1 - b) % wide, 1)
                for i in range(2):
                    at = 8 * (first + i) + s * 3 + b
                    put(shifts, at, 1, 1, moved[2 * s + i : 2 * s + i + 1])

    for step in range(1, groups_x):
        arrived_x(recv3, s3, r3, step)
    gath4[h] = halved(jnp.transpose(recv3[...].reshape(cols, 128))[: 2 * band], 0)
    pending += spread_y(gath4, s4, r4)

    def forward_row(i, carry):
        for j in range(2):
            n = 2 * i + j
            window = take(shifts, pl.multiple_of(8 * n, 8), 24)
            coarse = window.astype(bf16).astype(f32)
            window = jnp.concatenate([coarse, coarse, window - coarse, none], axis=0)
            tan = jnp.tanh(dot(mixed_b, window.astype(bf16)))
            tbuf[n] = tan.astype(bf16)
            slope[n] = (1.0 - tan * tan).astype(bf16)
        return carry

    lax.fori_loop(0, (rows + 2) // 2, forward_row, 0)

    loads[1].wait()
    field = jnp.zeros((2 * band, wide), f32)
    for step in range(groups_y):
        src = h if step == 0 else arrived_y(gath4, s4, r4, step)
        where = pl.ds(pl.multiple_of(src * cols, cols), cols)
        got = gath4[src]
        both_parts = dot(got, iy[0, where, :])
        field = field + both_parts[: 2 * band] + both_parts[2 * band :]
        field = field + dot(got[: 2 * band], iy[1, where, :])
    gp2[...] = jnp.zeros_like(gp2)
    for s in range(2):
        part = field[s * band : (s + 1) * band]
        put(gp2, 8 + s, rows, 8, part[:rows])
        put(gp2, 8 * (rows + 1) + s, 1, 1, part[rows : rows + 1])
        put(gp2, s, 1, 1, part[band - 1 :])

    def backward_row(n, own):
        gp8 = take(gp2, pl.multiple_of(8 * n, 8), 8)
        gp16 = jnp.concatenate([gp8, jnp.zeros_like(gp8)], axis=0).astype(bf16)
        tan = tbuf[n]
        gz = (dot(out_b, gp16, ((0,), (0,))) * slope[n].astype(f32)).astype(bf16)
        back = dot(back_b, jnp.concatenate([gz, gp16], axis=0))
        put(ubuf, pl.multiple_of(24 * n, 8), 24, 1, back)
        if not own:
            return None
        window = take(shifts, pl.multiple_of(8 * n, 8), 24, tiles=cols // 128)
        coarse = window.astype(bf16).astype(f32)
        pad = jnp.zeros_like(gp8[:, :cols])
        right_side = [window, gp8[:, :cols], window - coarse, pad]
        right_side = jnp.concatenate(right_side, axis=0).astype(bf16)
        left_side = jnp.concatenate([gz[:, :cols], tan[:, :cols], gp16[:, :cols]], axis=0)
        return dot(left_side, right_side, ((1,), (1,)))

    def backward_rows(i, total):
        for j in range(4):
            total = total + backward_row(1 + 4 * i + j, True)
        return total

    acc = lax.fori_loop(0, rows // 4, backward_rows, jnp.zeros((144, 64), f32))
    acc = acc[:, :32] + acc[:, 32:]

    low = lax.broadcasted_iota(jnp.int32, (64, 32), 1) < 24
    packed = jnp.concatenate(
        [jnp.where(low, acc[:64], acc[64:128]), acc[128:144], jnp.zeros((48, 32), f32)], axis=0
    )
    pay_y[h] = jnp.transpose(jnp.pad(packed, ((0, 0), (0, 96))))[:32]
    pending += spread_y(pay_y, s5, r5)

    backward_row(0, False)
    backward_row(rows + 1, False)
    for s in range(2):
        result = take(gp2, 8 + s, rows, 8)
        for b in range(3):
            k = s * 3 + b
            part = (
                take(ubuf, 48 + k, rows, 24)
                + take(ubuf, 24 + 8 + k, rows, 24)
                + take(ubuf, 16 + k, rows, 24)
            )
            if b != 1:
                part = pltpu.roll(part, (b - 1) % wide, 1)
            result = result + part
        gv_ref[s] = result[:, :cols]

    for step in range(1, groups_y):
        arrived_y(pay_y, s5, r5, step)
    summed = pay_y[0]
    for src in range(1, groups_y):
        summed = summed + pay_y[src]
    pay_x[w] = summed
    pending += spread_x(lambda dst: pay_x.at[w], pay_x, s6, r6)
    for step in range(1, groups_x):
        arrived_x(pay_x, s6, r6, step)
    sums = pay_x[0]
    for src in range(1, groups_x):
        sums = sums + pay_x[src]
    sums = sums * (1.0 / math.sqrt(length_x * length_y))
    turned = jnp.transpose(jnp.pad(sums, ((0, 96), (0, 0))))
    gz_sum = turned[:64, :24]
    pair = dot(turned[64:72, :32], sel_mid_ref[...], exact=True)[:2]
    depth = dot(point, gz_sum, ((0,), (0,)), exact=True)
    gpoint_ref[0] = dot(gz_sum, both, ((1,), (1,)), exact=True)
    gtaps_ref[0] = dot(depth * lift_wide, sel_taps_ref[...], ((1,), (1,)), exact=True)
    glift_ref[...] = dot(
        depth * taps_wide, sel_lift_ref[...], ((1,), (1,)), exact=True
    ) + dot(outw, pair, ((0,), (0,)), exact=True)
    gout_ref[...] = sums[24:26, :64] + dot(pair, lift_ref[...], ((1,), (1,)), exact=True)
    for copy in pending:
        copy.wait_send()


def fused(velocity, cotangent, lift_weight, depth_kernels, point_weights, out_weight):
    groups_y, groups_x = lax.axis_size("ha"), lax.axis_size("wa")
    _, rows, cols = velocity.shape
    channels = lift_weight.shape[0]
    length_x, length_y = groups_x * rows, groups_y * cols
    per = length_y // (groups_x * groups_y)
    wide = cols + 128
    tables = make_tables(groups_y, groups_x, rows, cols)
    bf16, f32 = jnp.bfloat16, jnp.float32
    vmem = pl.BlockSpec(memory_space=pltpu.VMEM)
    dma = pltpu.SemaphoreType.DMA
    return pl.pallas_call(
        functools.partial(fused_kernel, groups_y, groups_x, rows, cols),
        out_shape=(
            jax.ShapeDtypeStruct((2, rows, cols), f32),
            jax.ShapeDtypeStruct((channels, 2), f32),
            jax.ShapeDtypeStruct((1, channels, 9), f32),
            jax.ShapeDtypeStruct((1, channels, channels), f32),
            jax.ShapeDtypeStruct((2, channels), f32),
        ),
        in_specs=[vmem] * 9 + [pl.BlockSpec(memory_space=pl.ANY)] * 4,
        out_specs=(vmem,) * 5,
        scratch_shapes=[
            pltpu.VMEM((2, cols, length_y), bf16),
            pltpu.VMEM((2, length_y, wide), bf16),
            pltpu.VMEM((groups_x, 6 * rows, 2 * length_x), bf16),
            pltpu.VMEM((2, 2 * length_x, groups_x * 128), bf16),
            pltpu.VMEM((groups_y, 4 * rows, cols), bf16),
            pltpu.VMEM((groups_x, per, 4 * rows), bf16),
            pltpu.VMEM((groups_x, per, 4 * rows), bf16),
            pltpu.VMEM((groups_x, per, 128), f32),
            pltpu.VMEM((groups_x, per, 128), f32),
            pltpu.VMEM((groups_y, 4 * (rows + 8), cols), bf16),
            pltpu.VMEM((2, 2 * rows, 128), f32),
            pltpu.VMEM((2, 2 * rows, 128), f32),
            pltpu.VMEM((2, 8, wide), f32),
            pltpu.VMEM((2, 8, wide), f32),
            pltpu.VMEM((2 * rows, wide), f32),
            pltpu.VMEM((wide // 128, 8 * (rows + 4), 128), f32),
            pltpu.VMEM((rows + 2, channels, wide), bf16),
            pltpu.VMEM((rows + 2, channels, wide), bf16),
            pltpu.VMEM((wide // 128, 8 * (rows + 2), 128), f32),
            pltpu.VMEM((wide // 128, 24 * (rows + 2), 128), f32),
            pltpu.VMEM((groups_y, 32, 128), f32),
            pltpu.VMEM((groups_x, 32, 128), f32),
            dma((4,)),
            dma((groups_y,)),
            dma((groups_y,)),
            dma((groups_x,)),
            dma((groups_x,)),
            dma((groups_x,)),
            dma((groups_x,)),
            dma((groups_y,)),
            dma((groups_y,)),
            dma((2,)),
            dma((2,)),
            dma((2,)),
            dma((2,)),
            dma((groups_y,)),
            dma((groups_y,)),
            dma((groups_x,)),
            dma((groups_x,)),
        ],
        compiler_params=pltpu.CompilerParams(
            collective_id=0, has_side_effects=True, vmem_limit_bytes=48 * 1024 * 1024
        ),
    )(
        velocity,
        cotangent,
        lift_weight,
        depth_kernels,
        point_weights,
        out_weight,
        *[jnp.asarray(s) for s in selectors()],
        *[jnp.asarray(t) for t in tables],
    )


def either(velocity, cotangent, lift_weight, depth_kernels, point_weights, out_weight):
    groups_y, groups_x = lax.axis_size("ha"), lax.axis_size("wa")
    layers, channels, _ = depth_kernels.shape
    _, rows, cols = velocity.shape
    per = groups_y * cols // (groups_x * groups_y)
    fits = layers == 1 and channels == 64 and rows == 32 and cols % 256 == 0
    fits = fits and per % 32 == 0 and groups_y * cols <= 1024 and groups_x * rows == 256
    run = fused if fits else local
    return run(velocity, cotangent, lift_weight, depth_kernels, point_weights, out_weight)


def solution(mesh):
    return jax.shard_map(
        either,
        mesh=mesh,
        in_specs=(P(None, "wa", "ha"), P(None, "wa", "ha"), P(), P(), P(), P()),
        out_specs=(P(None, "wa", "ha"), P(), P(), P(), P()),
        check_vma=False,
    )
```

```python
import functools
import math

import jax
import jax.numpy as jnp
import ml_dtypes
import numpy as np
from jax import lax
from jax.experimental import pallas as pl
from jax.experimental.pallas import tpu as pltpu
from jax.sharding import PartitionSpec as P

OFFSETS = ((-1, -1), (-1, 0), (-1, 1), (0, -1), (0, 0), (0, 1), (1, -1), (1, 0), (1, 1))
TWO_PI = 2.0 * math.pi


def extended(value, sides, width):
    for axis, dim in sides:
        size, length = (lax.axis_size(axis), value.shape[dim])
        up = [(i, (i + 1) % size) for i in range(size)]
        down = [(j, i) for i, j in up]
        last = lax.slice_in_dim(value, length - width, length, axis=dim)
        leading = lax.slice_in_dim(value, 0, width, axis=dim)
        before = lax.ppermute(last, axis, up)
        after = lax.ppermute(leading, axis, down)
        value = jnp.concatenate([before, value, after], axis=dim)
    return value


def dft_table(table_len, sign_val):
    ids = jnp.arange(table_len, dtype=jnp.int32)
    product = ids[:, None] * ids[None, :] % table_len
    phase_angle = sign_val * TWO_PI / table_len * product.astype(jnp.float32)
    return (jnp.cos(phase_angle), jnp.sin(phase_angle))


def apply_table(values, tab_real, tab_imag):
    highest = lax.Precision.HIGHEST
    real_part = values[0]
    imag_part = values[1]
    out_real = jnp.einsum("...n,kn->...k", real_part, tab_real, precision=highest) - jnp.einsum(
        "...n,kn->...k", imag_part, tab_imag, precision=highest
    )
    out_imag = jnp.einsum("...n,kn->...k", real_part, tab_imag, precision=highest) + jnp.einsum(
        "...n,kn->...k", imag_part, tab_real, precision=highest
    )
    return jnp.stack([out_real, out_imag])


def rotate(values, phase_angle):
    cosine = jnp.cos(phase_angle)
    sine_val = jnp.sin(phase_angle)
    return jnp.stack(
        [values[0] * cosine - values[1] * sine_val, values[0] * sine_val + values[1] * cosine]
    )


def forward_first(values, axis_dim, groups, own_index, length):
    moved = jnp.moveaxis(values, axis_dim, -1)
    leading = moved.shape[:-1]
    full_len = moved.shape[-1]
    piece_len = full_len // groups
    moved = jnp.swapaxes(moved.reshape(leading + (groups, piece_len)), -1, -2)
    tab_real, tab_imag = dft_table(groups, -1.0)
    moved = apply_table(moved, tab_real, tab_imag)
    local_m = jnp.arange(piece_len, dtype=jnp.int32)[:, None] + own_index * piece_len
    first_k = jnp.arange(groups, dtype=jnp.int32)[None, :]
    phase_angle = -TWO_PI / length * (local_m * first_k % length).astype(jnp.float32)
    moved = rotate(moved, phase_angle)
    moved = jnp.swapaxes(moved, -1, -2).reshape(leading + (full_len,))
    return jnp.moveaxis(moved, -1, axis_dim)


def forward_second(values, axis_dim):
    moved = jnp.moveaxis(values, axis_dim, -1)
    tab_real, tab_imag = dft_table(moved.shape[-1], -1.0)
    moved = apply_table(moved, tab_real, tab_imag)
    return jnp.moveaxis(moved, -1, axis_dim)


def inverse_first(values, axis_dim, own_index, length):
    moved = jnp.moveaxis(values, axis_dim, -1)
    full_len = moved.shape[-1]
    tab_real, tab_imag = dft_table(full_len, 1.0)
    moved = apply_table(moved, tab_real, tab_imag)
    local_m = jnp.arange(full_len, dtype=jnp.int32)
    phase_angle = TWO_PI / length * (local_m * own_index % length).astype(jnp.float32)
    moved = rotate(moved, phase_angle)
    return jnp.moveaxis(moved, -1, axis_dim)


def inverse_second(values, axis_dim, groups):
    moved = jnp.moveaxis(values, axis_dim, -1)
    leading = moved.shape[:-1]
    full_len = moved.shape[-1]
    piece_len = full_len // groups
    moved = jnp.swapaxes(moved.reshape(leading + (groups, piece_len)), -1, -2)
    tab_real, tab_imag = dft_table(groups, 1.0)
    moved = apply_table(moved, tab_real, tab_imag)
    moved = jnp.swapaxes(moved, -1, -2).reshape(leading + (full_len,))
    return jnp.moveaxis(moved, -1, axis_dim)


def signed_waves(own_index, groups, count_n):
    ids = own_index + groups * jnp.arange(count_n, dtype=jnp.int32)
    total_len = groups * count_n
    return jnp.where(2 * ids >= total_len, ids - total_len, ids).astype(jnp.float32)


def project(spectrum, wave_x, wave_y):
    along_k = wave_x * spectrum[:, 0] + wave_y * spectrum[:, 1]
    factor = along_k / jnp.maximum(wave_x * wave_x + wave_y * wave_y, 1.0)
    return jnp.stack([spectrum[:, 0] - wave_x * factor, spectrum[:, 1] - wave_y * factor], axis=1)


def depthwise_valid(padded, kernel):
    rows_in = padded.shape[1] - 2
    cols_in = padded.shape[2] - 2
    total = jnp.zeros((padded.shape[0], rows_in, cols_in), jnp.float32)
    for offset_id in range(9):
        step_x, step_y = OFFSETS[offset_id]
        total = (
            total
            + kernel[:, offset_id][:, None, None]
            * padded[:, 1 + step_x : 1 + step_x + rows_in, 1 + step_y : 1 + step_y + cols_in]
        )
    return total


def transposed_add(grad_hidden, grad_pad, kernel):
    rows_in = grad_hidden.shape[1]
    cols_in = grad_hidden.shape[2]
    for offset_id in range(9):
        step_x, step_y = OFFSETS[offset_id]
        grad_hidden = (
            grad_hidden
            + kernel[:, offset_id][:, None, None]
            * grad_pad[:, 1 - step_x : 1 - step_x + rows_in, 1 - step_y : 1 - step_y + cols_in]
        )
    return grad_hidden


def kernel_grad(grad_depth, padded):
    rows_in = grad_depth.shape[1]
    cols_in = grad_depth.shape[2]
    grad_full = grad_depth.astype(jnp.float32)
    entries = []
    for offset_id in range(9):
        step_x, step_y = OFFSETS[offset_id]
        window = padded[
            :, 1 + step_x : 1 + step_x + rows_in, 1 + step_y : 1 + step_y + cols_in
        ].astype(jnp.float32)
        entries.append(jnp.sum(grad_full * window, axis=(1, 2)))
    return jnp.stack(entries, axis=1)


def local(velocity, cotangent, lift_weight, depth_kernels, point_weights, out_weight):
    highest = lax.Precision.HIGHEST
    layers = depth_kernels.shape[0]
    cols_n = velocity.shape[1]
    rows_n = velocity.shape[2]
    groups_x = lax.axis_size("wa")
    groups_y = lax.axis_size("ha")
    own_x = lax.axis_index("wa")
    own_y = lax.axis_index("ha")
    length_x = cols_n * groups_x
    length_y = rows_n * groups_y
    spectrum = jnp.stack([cotangent, jnp.zeros_like(cotangent)])
    wave_x = signed_waves(own_x, groups_x, cols_n)[:, None]
    wave_y = signed_waves(own_y, groups_y, rows_n)[None, :]

    def move_x(values):
        return lax.all_to_all(values, "wa", split_axis=2, concat_axis=2, tiled=True)

    def move_y(values):
        return lax.all_to_all(values, "ha", split_axis=3, concat_axis=3, tiled=True)

    spectrum = forward_first(move_x(spectrum), 2, groups_x, own_x, length_x)
    spectrum = forward_second(move_x(spectrum), 2)
    spectrum = forward_first(move_y(spectrum), 3, groups_y, own_y, length_y)
    spectrum = forward_second(move_y(spectrum), 3)
    spectrum = project(spectrum, wave_x, wave_y)
    spectrum = move_y(inverse_first(spectrum, 3, own_y, length_y))
    spectrum = move_y(inverse_second(spectrum, 3, groups_y))
    spectrum = move_x(inverse_first(spectrum, 2, own_x, length_x))
    spectrum = move_x(inverse_second(spectrum, 2, groups_x))
    grad_proj = spectrum[0] / float(length_x * length_y)
    saved_pad, saved_depth, saved_tanh = ([], [], [])
    hidden = jnp.einsum("cs,sxy->cxy", lift_weight, velocity, precision=highest).astype(
        jnp.bfloat16
    )
    layer_id = 0
    padded = extended(hidden, (("ha", 2), ("wa", 1)), 1)
    depth_out = depthwise_valid(padded, depth_kernels[layer_id]).astype(jnp.bfloat16)
    mixed_pre = jnp.einsum(
        "oc,cxy->oxy", point_weights[layer_id], depth_out, preferred_element_type=jnp.float32
    )
    squash = jnp.tanh(mixed_pre).astype(jnp.bfloat16)
    saved_pad.append(padded)
    saved_depth.append(depth_out)
    saved_tanh.append(squash)
    hidden = (hidden.astype(jnp.float32) + squash.astype(jnp.float32)).astype(jnp.bfloat16)
    grad_proj_b = grad_proj.astype(jnp.bfloat16)
    out_sum = jnp.einsum("sxy,cxy->sc", grad_proj_b, hidden, preferred_element_type=jnp.float32)
    grad_hidden = jnp.einsum(
        "sc,sxy->cxy", out_weight, grad_proj_b, preferred_element_type=jnp.float32
    )
    kernel_sums = [None] * layers
    point_sums = [None] * layers
    for layer_id in reversed(range(layers)):
        squash_full = saved_tanh[layer_id].astype(jnp.float32)
        grad_mixed = (grad_hidden * (1.0 - squash_full * squash_full)).astype(jnp.bfloat16)
        point_sums[layer_id] = jnp.einsum(
            "oxy,cxy->oc", grad_mixed, saved_depth[layer_id], preferred_element_type=jnp.float32
        )
        grad_depth = jnp.einsum(
            "oc,oxy->cxy", point_weights[layer_id], grad_mixed, preferred_element_type=jnp.float32
        ).astype(jnp.bfloat16)
        grad_pad = extended(grad_depth, (("ha", 2), ("wa", 1)), 1)
        kernel_sums[layer_id] = kernel_grad(grad_depth, saved_pad[layer_id])
        grad_hidden = transposed_add(grad_hidden, grad_pad, depth_kernels[layer_id])
    lift_sum = jnp.einsum("cxy,sxy->cs", grad_hidden, velocity, precision=highest)
    grad_velocity = grad_proj + jnp.einsum(
        "cs,cxy->sxy", lift_weight, grad_hidden, precision=highest
    )
    totals = lax.psum(
        (lift_sum, jnp.stack(kernel_sums), jnp.stack(point_sums), out_sum), ("ha", "wa")
    )
    scale = 1.0 / math.sqrt(length_x * length_y)
    return (
        grad_velocity,
        totals[0] * scale,
        totals[1] * scale,
        totals[2] * scale,
        totals[3] * scale,
    )


def real_basis(pairs, is_sin, positions, length):
    angle = 2.0 * np.pi / length * (np.outer(pairs, positions) % length)
    sines = np.where(pairs[:, None] == 0, np.cos(np.pi * positions)[None, :], np.sin(angle))
    return np.where(is_sin[:, None], sines, np.cos(angle))


def make_tables(groups_y, groups_x, rows, cols):
    length_x, length_y = groups_x * rows, groups_y * cols
    per = length_y // (groups_x * groups_y)
    half = per // 2
    ids = np.arange(length_y)
    pair_y = (ids // per) * half + ids % half
    sin_y = (ids % per) >= half
    forward_y = real_basis(pair_y, sin_y, np.arange(length_y), length_y)
    forward_y = forward_y.reshape(groups_y, cols, length_y)
    lanes = np.arange(cols + 128)
    local_y = np.where(lanes > cols, -1, lanes)
    keep_y = (lanes <= cols) | (lanes == cols + 127)
    inverse_y = np.stack(
        [
            real_basis(pair_y, sin_y, (h * cols + local_y) % length_y, length_y) * keep_y
            for h in range(groups_y)
        ]
    )
    kx = np.arange(length_x)
    pair_x = kx % (length_x // 2)
    sin_x = kx >= length_x // 2
    basis_x = real_basis(pair_x, sin_x, np.arange(length_x), length_x)
    forward_x = np.zeros((groups_x, 2, rows, 2, length_x))
    band = rows + 8
    inverse_x = np.zeros((2, length_x, groups_x, 128))
    local_x = np.arange(band)
    keep_x = (local_x <= rows) | (local_x == band - 1)
    local_x = np.where(local_x > rows, -1, local_x)
    for s in range(2):
        forward_x[:, s, :, s, :] = basis_x.T.reshape(groups_x, rows, length_x)
        for w in range(groups_x):
            part = basis_x[:, (w * rows + local_x) % length_x] * keep_x
            inverse_x[s, :, w, s * band : (s + 1) * band] = part
    forward_x = forward_x.reshape(groups_x, 2 * rows, 2 * length_x)
    inverse_x = inverse_x.reshape(2 * length_x, groups_x * 128)

    def halves(table, axis):
        coarse = table.astype(ml_dtypes.bfloat16)
        fine = (table - coarse.astype(np.float64)).astype(ml_dtypes.bfloat16)
        return np.stack([coarse, fine], axis=axis)

    forward_x = halves(forward_x, 1)
    forward_x = np.concatenate([forward_x[:, 0], forward_x[:, 0], forward_x[:, 1]], axis=1)
    return halves(forward_y, 1), halves(inverse_y, 1), forward_x, halves(inverse_x, 0)


def dot(a, b, dims=((1,), (0,))):
    return lax.dot_general(a, b, (dims, ((), ())), preferred_element_type=jnp.float32)


def put(ref, start, count, stride, value):
    for tile in range(ref.shape[0]):
        ref[tile, pl.ds(start, count, stride=stride), :] = value[:, tile * 128 : (tile + 1) * 128]


def take(ref, start, count, stride=1, tiles=None):
    rows = pl.ds(start, count, stride=stride)
    parts = [ref[tile, rows, :] for tile in range(tiles or ref.shape[0])]
    return jnp.concatenate(parts, axis=1)


def halved(value, axis):
    coarse = value.astype(jnp.bfloat16)
    fine = (value - coarse.astype(jnp.float32)).astype(jnp.bfloat16)
    return jnp.concatenate([coarse, fine], axis=axis)


def fused_kernel(
    groups_y,
    groups_x,
    rows,
    cols,
    vel_hbm,
    cot_hbm,
    lift_hbm,
    taps_hbm,
    point_hbm,
    outw_hbm,
    fy_hbm,
    iy_hbm,
    fx_hbm,
    ix_hbm,
    gv_ref,
    glift_ref,
    gtaps_ref,
    gpoint_ref,
    gout_ref,
    vel_ref,
    cot_ref,
    lift_ref,
    taps_ref,
    point_ref,
    outw_ref,
    fy,
    iy,
    fx,
    ix,
    gath,
    send2,
    recv2,
    send3,
    recv3,
    gath4,
    halo_out,
    halo_in,
    edge_out,
    edge_in,
    ext,
    shifts,
    tbuf,
    slope,
    gp2,
    ubuf,
    pay_y,
    pay_x,
    table_sem,
    s1,
    r1,
    s2,
    r2,
    s3,
    r3,
    s4,
    r4,
    sh,
    rh,
    se,
    re,
    s5,
    r5,
    s6,
    r6,
):
    bf16, f32 = jnp.bfloat16, jnp.float32
    h = lax.axis_index("ha")
    w = lax.axis_index("wa")
    length_x, length_y = groups_x * rows, groups_y * cols
    per = length_y // (groups_x * groups_y)
    half = per // 2
    wide = cols + 128
    band = rows + 8

    loads = [
        pltpu.make_async_copy(fy_hbm.at[h], fy, table_sem.at[0]),
        pltpu.make_async_copy(iy_hbm.at[h], iy, table_sem.at[1]),
        pltpu.make_async_copy(fx_hbm, fx, table_sem.at[2]),
        pltpu.make_async_copy(ix_hbm, ix, table_sem.at[3]),
    ]
    pairs = [
        (cot_hbm, cot_ref),
        (vel_hbm, vel_ref),
        (lift_hbm, lift_ref),
        (taps_hbm, taps_ref),
        (point_hbm, point_ref),
        (outw_hbm, outw_ref),
    ]
    small = [
        pltpu.make_async_copy(src, dst, table_sem.at[4 + i]) for i, (src, dst) in enumerate(pairs)
    ]
    for load in small + [loads[0], loads[2], loads[3], loads[1]]:
        load.start()

    def ha_peer(step):
        return lax.rem(h + step, groups_y)

    def wa_peer(step):
        return lax.rem(w + step, groups_x)

    barrier = pltpu.get_barrier_semaphore()
    for step in range(1, groups_y):
        pl.semaphore_signal(
            barrier, inc=1, device_id=(ha_peer(step), w), device_id_type=pl.DeviceIdType.MESH
        )
    for step in range(1, groups_x):
        pl.semaphore_signal(
            barrier, inc=1, device_id=(h, wa_peer(step)), device_id_type=pl.DeviceIdType.MESH
        )

    def remote(src, dst, send, recv, device):
        return pltpu.make_async_remote_copy(
            src_ref=src,
            dst_ref=dst,
            send_sem=send,
            recv_sem=recv,
            device_id=device,
            device_id_type=pl.DeviceIdType.MESH,
        )

    small[0].wait()
    gath[h] = halved(cot_ref[...].reshape(2 * rows, cols), 0)
    small[1].wait()
    vel = vel_ref[...].reshape(2 * rows, cols)
    halo_out[0] = vel[:, :128]
    halo_out[1] = vel[:, cols - 128 :]
    pl.semaphore_wait(barrier, groups_y + groups_x - 2)

    def spread_y(buf, send, recv):
        copies = []
        for step in range(1, groups_y):
            copy = remote(buf.at[h], buf.at[h], send.at[step], recv.at[h], (ha_peer(step), w))
            copy.start()
            copies.append(copy)
        return copies

    def arrived_y(buf, send, recv, step):
        src = ha_peer(step)
        remote(buf.at[src], buf.at[src], send.at[step], recv.at[src], (src, w)).wait_recv()
        return src

    def spread_x(src_of, buf, send, recv):
        copies = []
        for step in range(1, groups_x):
            dst = wa_peer(step)
            copy = remote(src_of(dst), buf.at[w], send.at[step], recv.at[w], (h, dst))
            copy.start()
            copies.append(copy)
        return copies

    def arrived_x(buf, send, recv, step):
        src = wa_peer(step)
        remote(buf.at[src], buf.at[src], send.at[step], recv.at[src], (h, src)).wait_recv()
        return src

    pending = spread_y(gath, s1, r1)
    left, right = (ha_peer(groups_y - 1), w), (ha_peer(1), w)
    halo = [
        remote(halo_out.at[0], halo_in.at[0], sh.at[0], rh.at[0], left),
        remote(halo_out.at[1], halo_in.at[1], sh.at[1], rh.at[1], right),
    ]
    for copy in halo:
        copy.start()

    for load in small[2:]:
        load.wait()
    lift = lift_ref[...]
    taps = taps_ref[:, 0, :]
    point = point_ref[0]
    outw = outw_ref[...].astype(f32)
    empty = jnp.zeros((2, lift.shape[1]), f32)
    lift_wide, taps_wide = [], []
    for a in range(3):
        for k in range(2):
            lift_wide += [lift[k : k + 1]] * 3
            taps_wide += [taps[3 * a : 3 * a + 3]]
        lift_wide.append(empty)
        taps_wide.append(empty)
    lift_wide = jnp.concatenate(lift_wide, axis=0)
    taps_wide = jnp.concatenate(taps_wide, axis=0)
    both = lift_wide * taps_wide
    mixed = dot(halved(both, 0), point, ((1,), (1,)))
    mixed = mixed[:24] + mixed[24:]
    coarse = mixed.astype(bf16).astype(f32)
    stack = [coarse, mixed - coarse, coarse, jnp.zeros((56, 64), f32)]
    stack = jnp.pad(jnp.concatenate(stack, axis=0), ((0, 0), (0, 64)))
    mixed_b = jnp.transpose(stack)[:64, :80].astype(bf16)
    none = jnp.zeros((8, wide), f32)
    out_pad = jnp.concatenate([outw, jnp.zeros((14, 64), f32)], axis=0)
    columns = jnp.transpose(jnp.pad(out_pad, ((0, 112), (0, 64))))
    out_0 = jnp.broadcast_to(columns[:64, 0:1], (64, wide))
    out_1 = jnp.broadcast_to(columns[:64, 1:2], (64, wide))
    lift_pad = jnp.concatenate([lift, jnp.zeros((6, 64), f32)], axis=0)
    through = dot(halved(lift_pad, 0), out_pad.astype(bf16), ((1,), (1,)))
    through = through[:8] + through[8:]
    row_24 = lax.broadcasted_iota(jnp.int32, (24, 16), 0)
    place = jnp.where(row_24 == 9, through[0:1], jnp.where(row_24 == 12, through[1:2], 0.0))
    back_b = jnp.concatenate([mixed, place], axis=1).astype(bf16)

    row_id = lax.broadcasted_iota(jnp.int32, (per, length_x), 0)
    lane_id = lax.broadcasted_iota(jnp.int32, (per, length_x), 1)
    py = (h * groups_x + w) * half + lax.rem(row_id, half)
    px = lax.rem(lane_id, length_x // 2)
    ysin, xsin = row_id >= half, lane_id >= length_x // 2
    ky = jnp.where((py == 0) & ysin, length_y // 2, py).astype(f32)
    kx = jnp.where((px == 0) & xsin, length_x // 2, px).astype(f32)
    weight = jnp.where(py == 0, 1.0, 2.0) * jnp.where(px == 0, 1.0, 2.0) / (length_x * length_y)
    inverse_k = weight / jnp.maximum(kx * kx + ky * ky, 1.0)
    keep_0 = weight - kx * kx * inverse_k
    keep_1 = weight - ky * ky * inverse_k
    cross = kx * ky * inverse_k
    inner = (px != 0) & (py != 0)
    turn = jnp.where(inner, jnp.where(ysin == xsin, -cross, cross), 0.0)
    corner = jnp.where((px == 0) & (py == 0) & ysin & xsin, cross, 0.0)

    loads[0].wait()
    spec = jnp.zeros((cols, 2 * rows), f32)
    for step in range(groups_y):
        src = h if step == 0 else arrived_y(gath, s1, r1, step)
        where = pl.ds(pl.multiple_of(src * cols, cols), cols)
        field = gath[src]
        both_parts = dot(fy[0, :, where], field, ((1,), (1,)))
        spec = spec + both_parts[:, : 2 * rows] + both_parts[:, 2 * rows :]
        spec = spec + dot(fy[1, :, where], field[: 2 * rows], ((1,), (1,)))
    send2[...] = halved(spec, 1).reshape(groups_x, per, 4 * rows)
    pending += spread_x(lambda dst: send2.at[dst], recv2, s2, r2)
    recv2[w] = send2[w]

    for copy in halo:
        copy.wait()
    side = lax.broadcasted_iota(jnp.int32, (2 * rows, 128), 1)
    tail = jnp.where(side < 64, halo_in[0], halo_in[1])
    ext[:, :cols] = vel
    ext[:, cols:] = tail
    edge_out[...] = jnp.zeros_like(edge_out)
    for s in range(2):
        edge_out[0, 2 * s : 2 * s + 2, :] = ext[s * rows : s * rows + 2, :]
        edge_out[1, 2 * s : 2 * s + 2, :] = ext[s * rows + rows - 2 : s * rows + rows, :]
    edges = [
        remote(edge_out.at[0], edge_in.at[0], se.at[0], re.at[0], (h, wa_peer(groups_x - 1))),
        remote(edge_out.at[1], edge_in.at[1], se.at[1], re.at[1], (h, wa_peer(1))),
    ]
    for copy in edges:
        copy.start()
    shifts[...] = jnp.zeros_like(shifts)
    for s in range(2):
        for b in range(3):
            moved = ext[s * rows : (s + 1) * rows, :]
            if b != 1:
                moved = pltpu.roll(moved, (1 - b) % wide, 1)
            put(shifts, 16 + s * 3 + b, rows, 8, moved)

    loads[2].wait()
    waves = jnp.zeros((per, 2 * length_x), f32)
    for step in range(groups_x):
        src = w if step == 0 else arrived_x(recv2, s2, r2, step)
        got = recv2[src]
        waves = waves + dot(jnp.concatenate([got, got[:, : 2 * rows]], axis=1), fx[src])
    a0, a1 = waves[:, :length_x], waves[:, length_x:]

    def swapped(a):
        a = jnp.concatenate([a[half:], a[:half]], axis=0)
        return jnp.concatenate([a[:, length_x // 2 :], a[:, : length_x // 2]], axis=1)

    p0 = keep_0 * a0 - turn * swapped(a1) - corner * a1
    p1 = keep_1 * a1 - turn * swapped(a0) - corner * a0
    loads[3].wait()
    split = halved(jnp.concatenate([p0, p1], axis=1), 0)
    fields = dot(split, ix[0])
    fields = fields[:per] + fields[per:] + dot(split[:per], ix[1])
    for dst in range(groups_x):
        send3[dst] = fields[:, dst * 128 : (dst + 1) * 128]
    pending += spread_x(lambda dst: send3.at[dst], recv3, s3, r3)
    recv3[w] = send3[w]

    for copy in edges:
        copy.wait()
    for s in range(2):
        for b in range(3):
            for slot, first in ((1, 0), (0, rows + 2)):
                moved = edge_in[slot]
                if b != 1:
                    moved = pltpu.roll(moved, (1 - b) % wide, 1)
                for i in range(2):
                    at = 8 * (first + i) + s * 3 + b
                    put(shifts, at, 1, 1, moved[2 * s + i : 2 * s + i + 1])

    for step in range(1, groups_x):
        arrived_x(recv3, s3, r3, step)
    gath4[h] = halved(jnp.transpose(recv3[...].reshape(cols, 128))[: 2 * band], 0)
    pending += spread_y(gath4, s4, r4)

    def forward_row(i, carry):
        for j in range(2):
            n = 2 * i + j
            window = take(shifts, pl.multiple_of(8 * n, 8), 24)
            coarse = window.astype(bf16).astype(f32)
            window = jnp.concatenate([coarse, coarse, window - coarse, none], axis=0)
            tan = jnp.tanh(dot(mixed_b, window.astype(bf16)))
            tbuf[n] = tan.astype(bf16)
            slope[n] = (1.0 - tan * tan).astype(bf16)
        return carry

    lax.fori_loop(0, (rows + 2) // 2, forward_row, 0)

    loads[1].wait()
    field = jnp.zeros((2 * band, wide), f32)
    for step in range(groups_y):
        src = h if step == 0 else arrived_y(gath4, s4, r4, step)
        where = pl.ds(pl.multiple_of(src * cols, cols), cols)
        got = gath4[src]
        both_parts = dot(got, iy[0, where, :])
        field = field + both_parts[: 2 * band] + both_parts[2 * band :]
        field = field + dot(got[: 2 * band], iy[1, where, :])
    gp2[...] = jnp.zeros_like(gp2)
    for s in range(2):
        part = field[s * band : (s + 1) * band]
        put(gp2, 8 + s, rows, 8, part[:rows])
        put(gp2, 8 * (rows + 1) + s, 1, 1, part[rows : rows + 1])
        put(gp2, s, 1, 1, part[band - 1 :])

    def backward_row(n, own):
        gp8 = take(gp2, pl.multiple_of(8 * n, 8), 8)
        gp16 = jnp.concatenate([gp8, jnp.zeros_like(gp8)], axis=0).astype(bf16)
        tan = tbuf[n]
        gpb = gp16.astype(f32)
        grad = out_0 * gpb[0:1] + out_1 * gpb[1:2]
        gz = (grad * slope[n].astype(f32)).astype(bf16)
        back = dot(back_b, jnp.concatenate([gz, gp16], axis=0))
        put(ubuf, pl.multiple_of(24 * n, 8), 24, 1, back)
        if not own:
            return None
        window = take(shifts, pl.multiple_of(8 * n, 8), 24, tiles=cols // 128)
        coarse = window.astype(bf16).astype(f32)
        pad = jnp.zeros_like(gp8[:, :cols])
        right_side = [window, gp8[:, :cols], window - coarse, pad]
        right_side = jnp.concatenate(right_side, axis=0).astype(bf16)
        left_side = jnp.concatenate([gz[:, :cols], tan[:, :cols], gp16[:, :cols]], axis=0)
        return dot(left_side, right_side, ((1,), (1,)))

    def backward_rows(i, total):
        for j in range(4):
            total = total + backward_row(1 + 4 * i + j, True)
        return total

    acc = lax.fori_loop(0, rows // 4, backward_rows, jnp.zeros((144, 64), f32))
    acc = acc[:, :32] + acc[:, 32:]

    low = lax.broadcasted_iota(jnp.int32, (64, 32), 1) < 24
    packed = jnp.concatenate(
        [jnp.where(low, acc[:64], acc[64:128]), acc[128:144], jnp.zeros((48, 32), f32)], axis=0
    )
    pay_y[h] = jnp.transpose(jnp.pad(packed, ((0, 0), (0, 96))))[:32]
    pending += spread_y(pay_y, s5, r5)

    backward_row(0, False)
    backward_row(rows + 1, False)
    for s in range(2):
        result = take(gp2, 8 + s, rows, 8)
        for b in range(3):
            k = s * 3 + b
            part = (
                take(ubuf, 48 + k, rows, 24)
                + take(ubuf, 24 + 8 + k, rows, 24)
                + take(ubuf, 16 + k, rows, 24)
            )
            if b != 1:
                part = pltpu.roll(part, (b - 1) % wide, 1)
            result = result + part
        gv_ref[s] = result[:, :cols]

    for step in range(1, groups_y):
        arrived_y(pay_y, s5, r5, step)
    summed = pay_y[0]
    for src in range(1, groups_y):
        summed = summed + pay_y[src]
    pay_x[w] = summed
    pending += spread_x(lambda dst: pay_x.at[w], pay_x, s6, r6)
    for step in range(1, groups_x):
        arrived_x(pay_x, s6, r6, step)
    sums = pay_x[0]
    for src in range(1, groups_x):
        sums = sums + pay_x[src]
    sums = sums * (1.0 / math.sqrt(length_x * length_y))
    gz_sum = sums[:24, :64]
    depth = dot(halved(gz_sum, 0), point)
    depth = depth[:24] + depth[24:]
    fine = gz_sum - gz_sum.astype(bf16).astype(f32)
    left_side = jnp.concatenate([gz_sum, fine, gz_sum, jnp.zeros((56, 64), f32)], axis=0)
    left_side = jnp.transpose(jnp.pad(left_side, ((0, 0), (0, 64))))[:64, :80].astype(bf16)
    fine = both - both.astype(bf16).astype(f32)
    right_side = jnp.concatenate([both, both, fine, jnp.zeros((8, 64), f32)], axis=0).astype(bf16)
    gpoint_ref[0] = dot(left_side, right_side)
    by_tap = depth * lift_wide
    by_lift = depth * taps_wide
    for a in range(3):
        for b in range(3):
            k = 8 * a + b
            gtaps_ref[3 * a + b] = by_tap[k : k + 1] + by_tap[k + 3 : k + 4]
    for s in range(2):
        total = jnp.zeros((1, 64), f32)
        for a in range(3):
            k = 8 * a + 3 * s
            total = total + jnp.sum(by_lift[k : k + 3], axis=0, keepdims=True)
        for r in range(2):
            total = total + sums[9 + 3 * s : 10 + 3 * s, 64 + r : 65 + r] * outw[r : r + 1]
        glift_ref[s : s + 1] = total
        total = sums[24 + s : 25 + s, :64]
        for r in range(2):
            total = total + sums[9 + 3 * r : 10 + 3 * r, 64 + s : 65 + s] * lift[r : r + 1]
        gout_ref[s : s + 1] = total
    for copy in pending:
        copy.wait_send()


def fused(velocity, cotangent, lift_weight, depth_kernels, point_weights, out_weight):
    groups_y, groups_x = lax.axis_size("ha"), lax.axis_size("wa")
    _, rows, cols = velocity.shape
    channels = lift_weight.shape[0]
    length_x, length_y = groups_x * rows, groups_y * cols
    per = length_y // (groups_x * groups_y)
    wide = cols + 128
    tables = make_tables(groups_y, groups_x, rows, cols)
    bf16, f32 = jnp.bfloat16, jnp.float32
    vmem = pl.BlockSpec(memory_space=pltpu.VMEM)
    dma = pltpu.SemaphoreType.DMA
    results = pl.pallas_call(
        functools.partial(fused_kernel, groups_y, groups_x, rows, cols),
        out_shape=(
            jax.ShapeDtypeStruct((2, rows, cols), f32),
            jax.ShapeDtypeStruct((2, channels), f32),
            jax.ShapeDtypeStruct((9, 1, channels), f32),
            jax.ShapeDtypeStruct((1, channels, channels), f32),
            jax.ShapeDtypeStruct((2, channels), f32),
        ),
        in_specs=[pl.BlockSpec(memory_space=pltpu.HBM)] * 10,
        out_specs=(vmem,) * 5,
        scratch_shapes=[
            pltpu.VMEM((2, rows, cols), f32),
            pltpu.VMEM((2, rows, cols), f32),
            pltpu.VMEM((2, channels), f32),
            pltpu.VMEM((9, 1, channels), f32),
            pltpu.VMEM((1, channels, channels), bf16),
            pltpu.VMEM((2, channels), bf16),
            pltpu.VMEM((2, cols, length_y), bf16),
            pltpu.VMEM((2, length_y, wide), bf16),
            pltpu.VMEM((groups_x, 6 * rows, 2 * length_x), bf16),
            pltpu.VMEM((2, 2 * length_x, groups_x * 128), bf16),
            pltpu.VMEM((groups_y, 4 * rows, cols), bf16),
            pltpu.VMEM((groups_x, per, 4 * rows), bf16),
            pltpu.VMEM((groups_x, per, 4 * rows), bf16),
            pltpu.VMEM((groups_x, per, 128), f32),
            pltpu.VMEM((groups_x, per, 128), f32),
            pltpu.VMEM((groups_y, 4 * (rows + 8), cols), bf16),
            pltpu.VMEM((2, 2 * rows, 128), f32),
            pltpu.VMEM((2, 2 * rows, 128), f32),
            pltpu.VMEM((2, 8, wide), f32),
            pltpu.VMEM((2, 8, wide), f32),
            pltpu.VMEM((2 * rows, wide), f32),
            pltpu.VMEM((wide // 128, 8 * (rows + 4), 128), f32),
            pltpu.VMEM((rows + 2, channels, wide), bf16),
            pltpu.VMEM((rows + 2, channels, wide), bf16),
            pltpu.VMEM((wide // 128, 8 * (rows + 2), 128), f32),
            pltpu.VMEM((wide // 128, 24 * (rows + 2), 128), f32),
            pltpu.VMEM((groups_y, 32, 128), f32),
            pltpu.VMEM((groups_x, 32, 128), f32),
            dma((10,)),
            dma((groups_y,)),
            dma((groups_y,)),
            dma((groups_x,)),
            dma((groups_x,)),
            dma((groups_x,)),
            dma((groups_x,)),
            dma((groups_y,)),
            dma((groups_y,)),
            dma((2,)),
            dma((2,)),
            dma((2,)),
            dma((2,)),
            dma((groups_y,)),
            dma((groups_y,)),
            dma((groups_x,)),
            dma((groups_x,)),
        ],
        compiler_params=pltpu.CompilerParams(
            collective_id=0, has_side_effects=True, vmem_limit_bytes=64 * 1024 * 1024
        ),
    )(
        velocity,
        cotangent,
        lift_weight.T,
        jnp.transpose(depth_kernels, (2, 0, 1)),
        point_weights,
        out_weight,
        *[jnp.asarray(t) for t in tables],
    )
    grad_velocity, grad_lift, grad_taps, grad_point, grad_out = results
    return grad_velocity, grad_lift.T, jnp.transpose(grad_taps, (1, 2, 0)), grad_point, grad_out


def either(velocity, cotangent, lift_weight, depth_kernels, point_weights, out_weight):
    groups_y, groups_x = lax.axis_size("ha"), lax.axis_size("wa")
    layers, channels, _ = depth_kernels.shape
    _, rows, cols = velocity.shape
    per = groups_y * cols // (groups_x * groups_y)
    fits = layers == 1 and channels == 64 and rows == 32 and cols % 256 == 0
    fits = fits and per % 32 == 0 and groups_y * cols <= 1024 and groups_x * rows == 256
    run = fused if fits else local
    return run(velocity, cotangent, lift_weight, depth_kernels, point_weights, out_weight)


def solution(mesh):
    return jax.shard_map(
        either,
        mesh=mesh,
        in_specs=(P(None, "wa", "ha"), P(None, "wa", "ha"), P(), P(), P(), P()),
        out_specs=(P(None, "wa", "ha"), P(), P(), P(), P()),
        check_vma=False,
    )
```

```python
import functools
import math

import jax
import jax.numpy as jnp
import ml_dtypes
import numpy as np
from jax import lax
from jax.experimental import pallas as pl
from jax.experimental.pallas import tpu as pltpu
from jax.sharding import PartitionSpec as P

OFFSETS = ((-1, -1), (-1, 0), (-1, 1), (0, -1), (0, 0), (0, 1), (1, -1), (1, 0), (1, 1))
TWO_PI = 2.0 * math.pi


def extended(value, sides, width):
    for axis, dim in sides:
        size, length = (lax.axis_size(axis), value.shape[dim])
        up = [(i, (i + 1) % size) for i in range(size)]
        down = [(j, i) for i, j in up]
        last = lax.slice_in_dim(value, length - width, length, axis=dim)
        leading = lax.slice_in_dim(value, 0, width, axis=dim)
        before = lax.ppermute(last, axis, up)
        after = lax.ppermute(leading, axis, down)
        value = jnp.concatenate([before, value, after], axis=dim)
    return value


def dft_table(table_len, sign_val):
    ids = jnp.arange(table_len, dtype=jnp.int32)
    product = ids[:, None] * ids[None, :] % table_len
    phase_angle = sign_val * TWO_PI / table_len * product.astype(jnp.float32)
    return (jnp.cos(phase_angle), jnp.sin(phase_angle))


def apply_table(values, tab_real, tab_imag):
    highest = lax.Precision.HIGHEST
    real_part = values[0]
    imag_part = values[1]
    out_real = jnp.einsum("...n,kn->...k", real_part, tab_real, precision=highest) - jnp.einsum(
        "...n,kn->...k", imag_part, tab_imag, precision=highest
    )
    out_imag = jnp.einsum("...n,kn->...k", real_part, tab_imag, precision=highest) + jnp.einsum(
        "...n,kn->...k", imag_part, tab_real, precision=highest
    )
    return jnp.stack([out_real, out_imag])


def rotate(values, phase_angle):
    cosine = jnp.cos(phase_angle)
    sine_val = jnp.sin(phase_angle)
    return jnp.stack(
        [values[0] * cosine - values[1] * sine_val, values[0] * sine_val + values[1] * cosine]
    )


def forward_first(values, axis_dim, groups, own_index, length):
    moved = jnp.moveaxis(values, axis_dim, -1)
    leading = moved.shape[:-1]
    full_len = moved.shape[-1]
    piece_len = full_len // groups
    moved = jnp.swapaxes(moved.reshape(leading + (groups, piece_len)), -1, -2)
    tab_real, tab_imag = dft_table(groups, -1.0)
    moved = apply_table(moved, tab_real, tab_imag)
    local_m = jnp.arange(piece_len, dtype=jnp.int32)[:, None] + own_index * piece_len
    first_k = jnp.arange(groups, dtype=jnp.int32)[None, :]
    phase_angle = -TWO_PI / length * (local_m * first_k % length).astype(jnp.float32)
    moved = rotate(moved, phase_angle)
    moved = jnp.swapaxes(moved, -1, -2).reshape(leading + (full_len,))
    return jnp.moveaxis(moved, -1, axis_dim)


def forward_second(values, axis_dim):
    moved = jnp.moveaxis(values, axis_dim, -1)
    tab_real, tab_imag = dft_table(moved.shape[-1], -1.0)
    moved = apply_table(moved, tab_real, tab_imag)
    return jnp.moveaxis(moved, -1, axis_dim)


def inverse_first(values, axis_dim, own_index, length):
    moved = jnp.moveaxis(values, axis_dim, -1)
    full_len = moved.shape[-1]
    tab_real, tab_imag = dft_table(full_len, 1.0)
    moved = apply_table(moved, tab_real, tab_imag)
    local_m = jnp.arange(full_len, dtype=jnp.int32)
    phase_angle = TWO_PI / length * (local_m * own_index % length).astype(jnp.float32)
    moved = rotate(moved, phase_angle)
    return jnp.moveaxis(moved, -1, axis_dim)


def inverse_second(values, axis_dim, groups):
    moved = jnp.moveaxis(values, axis_dim, -1)
    leading = moved.shape[:-1]
    full_len = moved.shape[-1]
    piece_len = full_len // groups
    moved = jnp.swapaxes(moved.reshape(leading + (groups, piece_len)), -1, -2)
    tab_real, tab_imag = dft_table(groups, 1.0)
    moved = apply_table(moved, tab_real, tab_imag)
    moved = jnp.swapaxes(moved, -1, -2).reshape(leading + (full_len,))
    return jnp.moveaxis(moved, -1, axis_dim)


def signed_waves(own_index, groups, count_n):
    ids = own_index + groups * jnp.arange(count_n, dtype=jnp.int32)
    total_len = groups * count_n
    return jnp.where(2 * ids >= total_len, ids - total_len, ids).astype(jnp.float32)


def project(spectrum, wave_x, wave_y):
    along_k = wave_x * spectrum[:, 0] + wave_y * spectrum[:, 1]
    factor = along_k / jnp.maximum(wave_x * wave_x + wave_y * wave_y, 1.0)
    return jnp.stack([spectrum[:, 0] - wave_x * factor, spectrum[:, 1] - wave_y * factor], axis=1)


def depthwise_valid(padded, kernel):
    rows_in = padded.shape[1] - 2
    cols_in = padded.shape[2] - 2
    total = jnp.zeros((padded.shape[0], rows_in, cols_in), jnp.float32)
    for offset_id in range(9):
        step_x, step_y = OFFSETS[offset_id]
        total = (
            total
            + kernel[:, offset_id][:, None, None]
            * padded[:, 1 + step_x : 1 + step_x + rows_in, 1 + step_y : 1 + step_y + cols_in]
        )
    return total


def transposed_add(grad_hidden, grad_pad, kernel):
    rows_in = grad_hidden.shape[1]
    cols_in = grad_hidden.shape[2]
    for offset_id in range(9):
        step_x, step_y = OFFSETS[offset_id]
        grad_hidden = (
            grad_hidden
            + kernel[:, offset_id][:, None, None]
            * grad_pad[:, 1 - step_x : 1 - step_x + rows_in, 1 - step_y : 1 - step_y + cols_in]
        )
    return grad_hidden


def kernel_grad(grad_depth, padded):
    rows_in = grad_depth.shape[1]
    cols_in = grad_depth.shape[2]
    grad_full = grad_depth.astype(jnp.float32)
    entries = []
    for offset_id in range(9):
        step_x, step_y = OFFSETS[offset_id]
        window = padded[
            :, 1 + step_x : 1 + step_x + rows_in, 1 + step_y : 1 + step_y + cols_in
        ].astype(jnp.float32)
        entries.append(jnp.sum(grad_full * window, axis=(1, 2)))
    return jnp.stack(entries, axis=1)


def local(velocity, cotangent, lift_weight, depth_kernels, point_weights, out_weight):
    highest = lax.Precision.HIGHEST
    layers = depth_kernels.shape[0]
    cols_n = velocity.shape[1]
    rows_n = velocity.shape[2]
    groups_x = lax.axis_size("wa")
    groups_y = lax.axis_size("ha")
    own_x = lax.axis_index("wa")
    own_y = lax.axis_index("ha")
    length_x = cols_n * groups_x
    length_y = rows_n * groups_y
    spectrum = jnp.stack([cotangent, jnp.zeros_like(cotangent)])
    wave_x = signed_waves(own_x, groups_x, cols_n)[:, None]
    wave_y = signed_waves(own_y, groups_y, rows_n)[None, :]

    def move_x(values):
        return lax.all_to_all(values, "wa", split_axis=2, concat_axis=2, tiled=True)

    def move_y(values):
        return lax.all_to_all(values, "ha", split_axis=3, concat_axis=3, tiled=True)

    spectrum = forward_first(move_x(spectrum), 2, groups_x, own_x, length_x)
    spectrum = forward_second(move_x(spectrum), 2)
    spectrum = forward_first(move_y(spectrum), 3, groups_y, own_y, length_y)
    spectrum = forward_second(move_y(spectrum), 3)
    spectrum = project(spectrum, wave_x, wave_y)
    spectrum = move_y(inverse_first(spectrum, 3, own_y, length_y))
    spectrum = move_y(inverse_second(spectrum, 3, groups_y))
    spectrum = move_x(inverse_first(spectrum, 2, own_x, length_x))
    spectrum = move_x(inverse_second(spectrum, 2, groups_x))
    grad_proj = spectrum[0] / float(length_x * length_y)
    saved_pad, saved_depth, saved_tanh = ([], [], [])
    hidden = jnp.einsum("cs,sxy->cxy", lift_weight, velocity, precision=highest).astype(
        jnp.bfloat16
    )
    layer_id = 0
    padded = extended(hidden, (("ha", 2), ("wa", 1)), 1)
    depth_out = depthwise_valid(padded, depth_kernels[layer_id]).astype(jnp.bfloat16)
    mixed_pre = jnp.einsum(
        "oc,cxy->oxy", point_weights[layer_id], depth_out, preferred_element_type=jnp.float32
    )
    squash = jnp.tanh(mixed_pre).astype(jnp.bfloat16)
    saved_pad.append(padded)
    saved_depth.append(depth_out)
    saved_tanh.append(squash)
    hidden = (hidden.astype(jnp.float32) + squash.astype(jnp.float32)).astype(jnp.bfloat16)
    grad_proj_b = grad_proj.astype(jnp.bfloat16)
    out_sum = jnp.einsum("sxy,cxy->sc", grad_proj_b, hidden, preferred_element_type=jnp.float32)
    grad_hidden = jnp.einsum(
        "sc,sxy->cxy", out_weight, grad_proj_b, preferred_element_type=jnp.float32
    )
    kernel_sums = [None] * layers
    point_sums = [None] * layers
    for layer_id in reversed(range(layers)):
        squash_full = saved_tanh[layer_id].astype(jnp.float32)
        grad_mixed = (grad_hidden * (1.0 - squash_full * squash_full)).astype(jnp.bfloat16)
        point_sums[layer_id] = jnp.einsum(
            "oxy,cxy->oc", grad_mixed, saved_depth[layer_id], preferred_element_type=jnp.float32
        )
        grad_depth = jnp.einsum(
            "oc,oxy->cxy", point_weights[layer_id], grad_mixed, preferred_element_type=jnp.float32
        ).astype(jnp.bfloat16)
        grad_pad = extended(grad_depth, (("ha", 2), ("wa", 1)), 1)
        kernel_sums[layer_id] = kernel_grad(grad_depth, saved_pad[layer_id])
        grad_hidden = transposed_add(grad_hidden, grad_pad, depth_kernels[layer_id])
    lift_sum = jnp.einsum("cxy,sxy->cs", grad_hidden, velocity, precision=highest)
    grad_velocity = grad_proj + jnp.einsum(
        "cs,cxy->sxy", lift_weight, grad_hidden, precision=highest
    )
    totals = lax.psum(
        (lift_sum, jnp.stack(kernel_sums), jnp.stack(point_sums), out_sum), ("ha", "wa")
    )
    scale = 1.0 / math.sqrt(length_x * length_y)
    return (
        grad_velocity,
        totals[0] * scale,
        totals[1] * scale,
        totals[2] * scale,
        totals[3] * scale,
    )


def real_basis(pairs, is_sin, positions, length):
    angle = 2.0 * np.pi / length * (np.outer(pairs, positions) % length)
    sines = np.where(pairs[:, None] == 0, np.cos(np.pi * positions)[None, :], np.sin(angle))
    return np.where(is_sin[:, None], sines, np.cos(angle))


def make_tables(groups_y, groups_x, rows, cols):
    length_x, length_y = groups_x * rows, groups_y * cols
    per = length_y // (groups_x * groups_y)
    half = per // 2
    ids = np.arange(length_y)
    pair_y = (ids // per) * half + ids % half
    sin_y = (ids % per) >= half
    forward_y = real_basis(pair_y, sin_y, np.arange(length_y), length_y)
    forward_y = forward_y.reshape(groups_y, cols, length_y)
    lanes = np.arange(cols + 128)
    local_y = np.where(lanes > cols, -1, lanes)
    keep_y = (lanes <= cols) | (lanes == cols + 127)
    inverse_y = np.stack(
        [
            real_basis(pair_y, sin_y, (h * cols + local_y) % length_y, length_y) * keep_y
            for h in range(groups_y)
        ]
    )
    kx = np.arange(length_x)
    pair_x = kx % (length_x // 2)
    sin_x = kx >= length_x // 2
    basis_x = real_basis(pair_x, sin_x, np.arange(length_x), length_x)
    forward_x = np.zeros((groups_x, 2, rows, 2, length_x))
    band = rows + 8
    inverse_x = np.zeros((2, length_x, groups_x, 128))
    local_x = np.arange(band)
    keep_x = (local_x <= rows) | (local_x == band - 1)
    local_x = np.where(local_x > rows, -1, local_x)
    for s in range(2):
        forward_x[:, s, :, s, :] = basis_x.T.reshape(groups_x, rows, length_x)
        for w in range(groups_x):
            part = basis_x[:, (w * rows + local_x) % length_x] * keep_x
            inverse_x[s, :, w, s * band : (s + 1) * band] = part
    forward_x = forward_x.reshape(groups_x, 2 * rows, 2 * length_x)
    inverse_x = inverse_x.reshape(2 * length_x, groups_x * 128)

    def halves(table, axis):
        coarse = table.astype(ml_dtypes.bfloat16)
        fine = (table - coarse.astype(np.float64)).astype(ml_dtypes.bfloat16)
        return np.stack([coarse, fine], axis=axis)

    forward_x = halves(forward_x, 1)
    forward_x = np.concatenate([forward_x[:, 0], forward_x[:, 0], forward_x[:, 1]], axis=1)
    return halves(forward_y, 1), halves(inverse_y, 1), forward_x, halves(inverse_x, 0)


def dot(a, b, dims=((1,), (0,))):
    return lax.dot_general(a, b, (dims, ((), ())), preferred_element_type=jnp.float32)


def put(ref, start, count, stride, value):
    for tile in range(ref.shape[0]):
        ref[tile, pl.ds(start, count, stride=stride), :] = value[:, tile * 128 : (tile + 1) * 128]


def take(ref, start, count, stride=1, tiles=None):
    rows = pl.ds(start, count, stride=stride)
    parts = [ref[tile, rows, :] for tile in range(tiles or ref.shape[0])]
    return jnp.concatenate(parts, axis=1)


def halved(value, axis):
    coarse = value.astype(jnp.bfloat16)
    fine = (value - coarse.astype(jnp.float32)).astype(jnp.bfloat16)
    return jnp.concatenate([coarse, fine], axis=axis)


def fused_kernel(
    groups_y,
    groups_x,
    rows,
    cols,
    vel_hbm,
    cot_hbm,
    lift_hbm,
    taps_hbm,
    point_hbm,
    outw_hbm,
    fy_hbm,
    iy_hbm,
    fx_hbm,
    ix_hbm,
    gv_ref,
    glift_ref,
    gtaps_ref,
    gpoint_ref,
    gout_ref,
    vel_ref,
    cot_ref,
    lift_ref,
    taps_ref,
    point_ref,
    outw_ref,
    fy,
    iy,
    fx,
    ix,
    gath,
    send2,
    recv2,
    send3,
    recv3,
    gath4,
    halo_out,
    halo_in,
    edge_out,
    edge_in,
    ext,
    shifts,
    tbuf,
    slope,
    gp2,
    ubuf,
    pay_y,
    pay_x,
    table_sem,
    s1,
    r1,
    s2,
    r2,
    s3,
    r3,
    s4,
    r4,
    sh,
    rh,
    se,
    re,
    s5,
    r5,
    s6,
    r6,
):
    bf16, f32 = jnp.bfloat16, jnp.float32
    h = lax.axis_index("ha")
    w = lax.axis_index("wa")
    length_x, length_y = groups_x * rows, groups_y * cols
    per = length_y // (groups_x * groups_y)
    half = per // 2
    wide = cols + 128
    band = rows + 8

    loads = [
        pltpu.make_async_copy(fy_hbm.at[h], fy, table_sem.at[0]),
        pltpu.make_async_copy(iy_hbm.at[h], iy, table_sem.at[1]),
        pltpu.make_async_copy(fx_hbm, fx, table_sem.at[2]),
        pltpu.make_async_copy(ix_hbm, ix, table_sem.at[3]),
    ]
    pairs = [
        (cot_hbm, cot_ref),
        (vel_hbm, vel_ref),
        (lift_hbm, lift_ref),
        (taps_hbm, taps_ref),
        (point_hbm, point_ref),
        (outw_hbm, outw_ref),
    ]
    small = [
        pltpu.make_async_copy(src, dst, table_sem.at[4 + i]) for i, (src, dst) in enumerate(pairs)
    ]
    for load in small + [loads[0], loads[2], loads[3], loads[1]]:
        load.start()

    def ha_peer(step):
        return lax.rem(h + step, groups_y)

    def wa_peer(step):
        return lax.rem(w + step, groups_x)

    barrier = pltpu.get_barrier_semaphore()
    for step in range(1, groups_y):
        pl.semaphore_signal(
            barrier, inc=1, device_id=(ha_peer(step), w), device_id_type=pl.DeviceIdType.MESH
        )
    for step in range(1, groups_x):
        pl.semaphore_signal(
            barrier, inc=1, device_id=(h, wa_peer(step)), device_id_type=pl.DeviceIdType.MESH
        )

    def remote(src, dst, send, recv, device):
        return pltpu.make_async_remote_copy(
            src_ref=src,
            dst_ref=dst,
            send_sem=send,
            recv_sem=recv,
            device_id=device,
            device_id_type=pl.DeviceIdType.MESH,
        )

    small[0].wait()
    gath[h] = halved(cot_ref[...].reshape(2 * rows, cols), 0)
    small[1].wait()
    vel = vel_ref[...].reshape(2 * rows, cols)
    halo_out[0] = vel[:, :128]
    halo_out[1] = vel[:, cols - 128 :]
    pl.semaphore_wait(barrier, groups_y + groups_x - 2)

    def spread_y(buf, send, recv):
        copies = []
        for step in range(1, groups_y):
            copy = remote(buf.at[h], buf.at[h], send.at[step], recv.at[h], (ha_peer(step), w))
            copy.start()
            copies.append(copy)
        return copies

    def arrived_y(buf, send, recv, step):
        src = ha_peer(step)
        remote(buf.at[src], buf.at[src], send.at[step], recv.at[src], (src, w)).wait_recv()
        return src

    def spread_x(src_of, buf, send, recv):
        copies = []
        for step in range(1, groups_x):
            dst = wa_peer(step)
            copy = remote(src_of(dst), buf.at[w], send.at[step], recv.at[w], (h, dst))
            copy.start()
            copies.append(copy)
        return copies

    def arrived_x(buf, send, recv, step):
        src = wa_peer(step)
        remote(buf.at[src], buf.at[src], send.at[step], recv.at[src], (h, src)).wait_recv()
        return src

    pending = spread_y(gath, s1, r1)
    left, right = (ha_peer(groups_y - 1), w), (ha_peer(1), w)
    halo = [
        remote(halo_out.at[0], halo_in.at[0], sh.at[0], rh.at[0], left),
        remote(halo_out.at[1], halo_in.at[1], sh.at[1], rh.at[1], right),
    ]
    for copy in halo:
        copy.start()

    for load in small[2:]:
        load.wait()
    lift = lift_ref[...]
    taps = taps_ref[:, 0, :]
    point = point_ref[0]
    outw = outw_ref[...].astype(f32)
    empty = jnp.zeros((2, lift.shape[1]), f32)
    lift_wide, taps_wide = [], []
    for a in range(3):
        for k in range(2):
            lift_wide += [lift[k : k + 1]] * 3
            taps_wide += [taps[3 * a : 3 * a + 3]]
        lift_wide.append(empty)
        taps_wide.append(empty)
    lift_wide = jnp.concatenate(lift_wide, axis=0)
    taps_wide = jnp.concatenate(taps_wide, axis=0)
    both = lift_wide * taps_wide
    mixed = dot(halved(both, 0), point, ((1,), (1,)))
    mixed = mixed[:24] + mixed[24:]
    coarse = mixed.astype(bf16).astype(f32)
    stack = [coarse, mixed - coarse, coarse, jnp.zeros((56, 64), f32)]
    stack = jnp.pad(jnp.concatenate(stack, axis=0), ((0, 0), (0, 64)))
    mixed_b = jnp.transpose(stack)[:64, :80].astype(bf16)
    none = jnp.zeros((8, wide), f32)
    out_pad = jnp.concatenate([outw, jnp.zeros((14, 64), f32)], axis=0)
    columns = jnp.transpose(jnp.pad(out_pad, ((0, 112), (0, 64))))
    out_0 = jnp.broadcast_to(columns[:64, 0:1], (64, wide))
    out_1 = jnp.broadcast_to(columns[:64, 1:2], (64, wide))
    lift_pad = jnp.concatenate([lift, jnp.zeros((6, 64), f32)], axis=0)
    through = dot(halved(lift_pad, 0), out_pad.astype(bf16), ((1,), (1,)))
    through = through[:8] + through[8:]
    row_24 = lax.broadcasted_iota(jnp.int32, (24, 16), 0)
    place = jnp.where(row_24 == 9, through[0:1], jnp.where(row_24 == 12, through[1:2], 0.0))
    back_b = jnp.concatenate([mixed, place], axis=1).astype(bf16)

    row_id = lax.broadcasted_iota(jnp.int32, (per, length_x), 0)
    lane_id = lax.broadcasted_iota(jnp.int32, (per, length_x), 1)
    py = (h * groups_x + w) * half + lax.rem(row_id, half)
    px = lax.rem(lane_id, length_x // 2)
    ysin, xsin = row_id >= half, lane_id >= length_x // 2
    ky = jnp.where((py == 0) & ysin, length_y // 2, py).astype(f32)
    kx = jnp.where((px == 0) & xsin, length_x // 2, px).astype(f32)
    weight = jnp.where(py == 0, 1.0, 2.0) * jnp.where(px == 0, 1.0, 2.0) / (length_x * length_y)
    inverse_k = weight / jnp.maximum(kx * kx + ky * ky, 1.0)
    keep_0 = weight - kx * kx * inverse_k
    keep_1 = weight - ky * ky * inverse_k
    cross = kx * ky * inverse_k
    inner = (px != 0) & (py != 0)
    turn = jnp.where(inner, jnp.where(ysin == xsin, -cross, cross), 0.0)
    corner = jnp.where((px == 0) & (py == 0) & ysin & xsin, cross, 0.0)

    loads[0].wait()
    spec = jnp.zeros((cols, 2 * rows), f32)
    for step in range(groups_y):
        src = h if step == 0 else arrived_y(gath, s1, r1, step)
        where = pl.ds(pl.multiple_of(src * cols, cols), cols)
        field = gath[src]
        both_parts = dot(fy[0, :, where], field, ((1,), (1,)))
        spec = spec + both_parts[:, : 2 * rows] + both_parts[:, 2 * rows :]
        spec = spec + dot(fy[1, :, where], field[: 2 * rows], ((1,), (1,)))
    send2[...] = halved(spec, 1).reshape(groups_x, per, 4 * rows)
    pending += spread_x(lambda dst: send2.at[dst], recv2, s2, r2)
    recv2[w] = send2[w]

    for copy in halo:
        copy.wait()
    side = lax.broadcasted_iota(jnp.int32, (2 * rows, 128), 1)
    tail = jnp.where(side < 64, halo_in[0], halo_in[1])
    ext[:, :cols] = vel
    ext[:, cols:] = tail
    edge_out[...] = jnp.zeros_like(edge_out)
    for s in range(2):
        edge_out[0, 2 * s : 2 * s + 2, :] = ext[s * rows : s * rows + 2, :]
        edge_out[1, 2 * s : 2 * s + 2, :] = ext[s * rows + rows - 2 : s * rows + rows, :]
    edges = [
        remote(edge_out.at[0], edge_in.at[0], se.at[0], re.at[0], (h, wa_peer(groups_x - 1))),
        remote(edge_out.at[1], edge_in.at[1], se.at[1], re.at[1], (h, wa_peer(1))),
    ]
    for copy in edges:
        copy.start()
    shifts[...] = jnp.zeros_like(shifts)
    for s in range(2):
        for b in range(3):
            moved = ext[s * rows : (s + 1) * rows, :]
            if b != 1:
                moved = pltpu.roll(moved, (1 - b) % wide, 1)
            put(shifts, 16 + s * 3 + b, rows, 8, moved)

    def forward_row(n):
        start = n * 8 if isinstance(n, int) else pl.multiple_of(8 * n, 8)
        window = take(shifts, start, 24)
        coarse = window.astype(bf16).astype(f32)
        window = jnp.concatenate([coarse, coarse, window - coarse, none], axis=0)
        tan = jnp.tanh(dot(mixed_b, window.astype(bf16)))
        tbuf[n] = tan.astype(bf16)
        slope[n] = (1.0 - tan * tan).astype(bf16)

    def forward_rows(first, count):
        def two(i, carry):
            forward_row(first + 2 * i)
            forward_row(first + 2 * i + 1)
            return carry

        lax.fori_loop(0, count // 2, two, 0)

    forward_rows(2, 4)

    loads[2].wait()
    waves = jnp.zeros((per, 2 * length_x), f32)
    for step in range(groups_x):
        src = w if step == 0 else arrived_x(recv2, s2, r2, step)
        got = recv2[src]
        waves = waves + dot(jnp.concatenate([got, got[:, : 2 * rows]], axis=1), fx[src])
    a0, a1 = waves[:, :length_x], waves[:, length_x:]

    def swapped(a):
        a = jnp.concatenate([a[half:], a[:half]], axis=0)
        return jnp.concatenate([a[:, length_x // 2 :], a[:, : length_x // 2]], axis=1)

    p0 = keep_0 * a0 - turn * swapped(a1) - corner * a1
    p1 = keep_1 * a1 - turn * swapped(a0) - corner * a0
    loads[3].wait()
    split = halved(jnp.concatenate([p0, p1], axis=1), 0)
    fields = dot(split, ix[0])
    fields = (fields[:per] + fields[per:] + dot(split[:per], ix[1])).astype(bf16)
    for dst in range(groups_x):
        send3[dst] = fields[:, dst * 128 : (dst + 1) * 128]
    pending += spread_x(lambda dst: send3.at[dst], recv3, s3, r3)
    recv3[w] = send3[w]

    forward_rows(6, 10)
    for copy in edges:
        copy.wait()
    for s in range(2):
        for b in range(3):
            for slot, first in ((1, 0), (0, rows + 2)):
                moved = edge_in[slot]
                if b != 1:
                    moved = pltpu.roll(moved, (1 - b) % wide, 1)
                for i in range(2):
                    at = 8 * (first + i) + s * 3 + b
                    put(shifts, at, 1, 1, moved[2 * s + i : 2 * s + i + 1])

    for step in range(1, groups_x):
        arrived_x(recv3, s3, r3, step)
    turned = jnp.transpose(recv3[...].reshape(cols, 128).astype(f32))
    gath4[h] = turned[: 2 * band].astype(bf16)
    pending += spread_y(gath4, s4, r4)

    forward_rows(16, rows - 16)
    for n in (0, 1, rows, rows + 1):
        forward_row(n)
    loads[1].wait()
    field = jnp.zeros((2 * band, wide), f32)
    for step in range(groups_y):
        src = h if step == 0 else arrived_y(gath4, s4, r4, step)
        where = pl.ds(pl.multiple_of(src * cols, cols), cols)
        got = gath4[src]
        field = field + dot(got, iy[0, where, :]) + dot(got, iy[1, where, :])
    gp2[...] = jnp.zeros_like(gp2)
    for s in range(2):
        part = field[s * band : (s + 1) * band]
        put(gp2, 8 + s, rows, 8, part[:rows])
        put(gp2, 8 * (rows + 1) + s, 1, 1, part[rows : rows + 1])
        put(gp2, s, 1, 1, part[band - 1 :])

    def backward_row(n, own):
        gp8 = take(gp2, pl.multiple_of(8 * n, 8), 8)
        gp16 = jnp.concatenate([gp8, jnp.zeros_like(gp8)], axis=0).astype(bf16)
        tan = tbuf[n]
        gpb = gp16.astype(f32)
        grad = out_0 * gpb[0:1] + out_1 * gpb[1:2]
        gz = (grad * slope[n].astype(f32)).astype(bf16)
        back = dot(back_b, jnp.concatenate([gz, gp16], axis=0))
        put(ubuf, pl.multiple_of(24 * n, 8), 24, 1, back)
        if not own:
            return None
        window = take(shifts, pl.multiple_of(8 * n, 8), 24, tiles=cols // 128)
        coarse = window.astype(bf16).astype(f32)
        pad = jnp.zeros_like(gp8[:, :cols])
        right_side = [window, gp8[:, :cols], window - coarse, pad]
        right_side = jnp.concatenate(right_side, axis=0).astype(bf16)
        left_side = jnp.concatenate([gz[:, :cols], tan[:, :cols], gp16[:, :cols]], axis=0)
        return dot(left_side, right_side, ((1,), (1,)))

    def backward_rows(i, total):
        for j in range(4):
            total = total + backward_row(1 + 4 * i + j, True)
        return total

    acc = lax.fori_loop(0, rows // 4, backward_rows, jnp.zeros((144, 64), f32))
    acc = acc[:, :32] + acc[:, 32:]

    low = lax.broadcasted_iota(jnp.int32, (64, 32), 1) < 24
    packed = jnp.concatenate(
        [jnp.where(low, acc[:64], acc[64:128]), acc[128:144], jnp.zeros((48, 32), f32)], axis=0
    )
    packed = jnp.transpose(jnp.pad(packed, ((0, 0), (0, 96))))[:32]
    upper = [packed[16:26, :64], packed[9:10, 64:], packed[12:13, 64:], packed[28:32, :64]]
    upper = jnp.concatenate(upper, axis=0)
    pay_y[h] = jnp.concatenate([packed[:16, :64], upper], axis=1)
    pending += spread_y(pay_y, s5, r5)

    backward_row(0, False)
    backward_row(rows + 1, False)
    for s in range(2):
        result = take(gp2, 8 + s, rows, 8)
        for b in range(3):
            k = s * 3 + b
            part = (
                take(ubuf, 48 + k, rows, 24)
                + take(ubuf, 24 + 8 + k, rows, 24)
                + take(ubuf, 16 + k, rows, 24)
            )
            if b != 1:
                part = pltpu.roll(part, (b - 1) % wide, 1)
            result = result + part
        gv_ref[s] = result[:, :cols]

    for step in range(1, groups_y):
        arrived_y(pay_y, s5, r5, step)
    summed = pay_y[0]
    for src in range(1, groups_y):
        summed = summed + pay_y[src]
    pay_x[w] = summed
    pending += spread_x(lambda dst: pay_x.at[w], pay_x, s6, r6)
    for step in range(1, groups_x):
        arrived_x(pay_x, s6, r6, step)
    sums = pay_x[0]
    for src in range(1, groups_x):
        sums = sums + pay_x[src]
    sums = sums * (1.0 / math.sqrt(length_x * length_y))
    gz_sum = jnp.concatenate([sums[:, :64], sums[:8, 64:]], axis=0)
    depth = dot(halved(gz_sum, 0), point)
    depth = depth[:24] + depth[24:]
    fine = gz_sum - gz_sum.astype(bf16).astype(f32)
    left_side = jnp.concatenate([gz_sum, fine, gz_sum, jnp.zeros((56, 64), f32)], axis=0)
    left_side = jnp.transpose(jnp.pad(left_side, ((0, 0), (0, 64))))[:64, :80].astype(bf16)
    fine = both - both.astype(bf16).astype(f32)
    right_side = jnp.concatenate([both, both, fine, jnp.zeros((8, 64), f32)], axis=0).astype(bf16)
    gpoint_ref[0] = dot(left_side, right_side)
    by_tap = depth * lift_wide
    by_lift = depth * taps_wide
    for a in range(3):
        for b in range(3):
            k = 8 * a + b
            gtaps_ref[3 * a + b] = by_tap[k : k + 1] + by_tap[k + 3 : k + 4]
    for s in range(2):
        total = jnp.zeros((1, 64), f32)
        for a in range(3):
            k = 8 * a + 3 * s
            total = total + jnp.sum(by_lift[k : k + 3], axis=0, keepdims=True)
        for r in range(2):
            total = total + sums[10 + s : 11 + s, 64 + r : 65 + r] * outw[r : r + 1]
        glift_ref[s : s + 1] = total
        total = sums[8 + s : 9 + s, 64:]
        for r in range(2):
            total = total + sums[10 + r : 11 + r, 64 + s : 65 + s] * lift[r : r + 1]
        gout_ref[s : s + 1] = total
    for copy in pending:
        copy.wait_send()


def hand_over(*refs):
    sources, targets, sems = refs[:5], refs[5:10], refs[10]
    copies = [pltpu.make_async_copy(sources[i], targets[i], sems.at[i]) for i in range(5)]
    for copy in copies:
        copy.start()
    for copy in copies:
        copy.wait()


def fused(velocity, cotangent, lift_weight, depth_kernels, point_weights, out_weight):
    groups_y, groups_x = lax.axis_size("ha"), lax.axis_size("wa")
    _, rows, cols = velocity.shape
    channels = lift_weight.shape[0]
    length_x, length_y = groups_x * rows, groups_y * cols
    per = length_y // (groups_x * groups_y)
    wide = cols + 128
    tables = make_tables(groups_y, groups_x, rows, cols)
    bf16, f32 = jnp.bfloat16, jnp.float32
    vmem = pl.BlockSpec(memory_space=pltpu.VMEM)
    dma = pltpu.SemaphoreType.DMA
    results = pl.pallas_call(
        functools.partial(fused_kernel, groups_y, groups_x, rows, cols),
        out_shape=(
            jax.ShapeDtypeStruct((2, rows, cols), f32),
            jax.ShapeDtypeStruct((2, channels), f32),
            jax.ShapeDtypeStruct((9, 1, channels), f32),
            jax.ShapeDtypeStruct((1, channels, channels), f32),
            jax.ShapeDtypeStruct((2, channels), f32),
        ),
        in_specs=[pl.BlockSpec(memory_space=pltpu.HBM)] * 10,
        out_specs=(vmem,) * 5,
        scratch_shapes=[
            pltpu.VMEM((2, rows, cols), f32),
            pltpu.VMEM((2, rows, cols), f32),
            pltpu.VMEM((2, channels), f32),
            pltpu.VMEM((9, 1, channels), f32),
            pltpu.VMEM((1, channels, channels), bf16),
            pltpu.VMEM((2, channels), bf16),
            pltpu.VMEM((2, cols, length_y), bf16),
            pltpu.VMEM((2, length_y, wide), bf16),
            pltpu.VMEM((groups_x, 6 * rows, 2 * length_x), bf16),
            pltpu.VMEM((2, 2 * length_x, groups_x * 128), bf16),
            pltpu.VMEM((groups_y, 4 * rows, cols), bf16),
            pltpu.VMEM((groups_x, per, 4 * rows), bf16),
            pltpu.VMEM((groups_x, per, 4 * rows), bf16),
            pltpu.VMEM((groups_x, per, 128), bf16),
            pltpu.VMEM((groups_x, per, 128), bf16),
            pltpu.VMEM((groups_y, 2 * (rows + 8), cols), bf16),
            pltpu.VMEM((2, 2 * rows, 128), f32),
            pltpu.VMEM((2, 2 * rows, 128), f32),
            pltpu.VMEM((2, 8, wide), f32),
            pltpu.VMEM((2, 8, wide), f32),
            pltpu.VMEM((2 * rows, wide), f32),
            pltpu.VMEM((wide // 128, 8 * (rows + 4), 128), f32),
            pltpu.VMEM((rows + 2, channels, wide), bf16),
            pltpu.VMEM((rows + 2, channels, wide), bf16),
            pltpu.VMEM((wide // 128, 8 * (rows + 2), 128), f32),
            pltpu.VMEM((wide // 128, 24 * (rows + 2), 128), f32),
            pltpu.VMEM((groups_y, 16, 128), f32),
            pltpu.VMEM((groups_x, 16, 128), f32),
            dma((10,)),
            dma((groups_y,)),
            dma((groups_y,)),
            dma((groups_x,)),
            dma((groups_x,)),
            dma((groups_x,)),
            dma((groups_x,)),
            dma((groups_y,)),
            dma((groups_y,)),
            dma((2,)),
            dma((2,)),
            dma((2,)),
            dma((2,)),
            dma((groups_y,)),
            dma((groups_y,)),
            dma((groups_x,)),
            dma((groups_x,)),
        ],
        compiler_params=pltpu.CompilerParams(
            collective_id=0, has_side_effects=True, vmem_limit_bytes=64 * 1024 * 1024
        ),
    )(
        velocity,
        cotangent,
        lift_weight.T,
        jnp.transpose(depth_kernels, (2, 0, 1)),
        point_weights,
        out_weight,
        *[jnp.asarray(t) for t in tables],
    )
    results = pl.pallas_call(
        hand_over,
        out_shape=[jax.ShapeDtypeStruct(r.shape, r.dtype) for r in results],
        in_specs=[pl.BlockSpec(memory_space=pltpu.HBM)] * 5,
        out_specs=[pl.BlockSpec(memory_space=pltpu.HBM)] * 5,
        scratch_shapes=[dma((5,))],
        compiler_params=pltpu.CompilerParams(vmem_limit_bytes=64 * 1024 * 1024),
    )(*results)
    grad_velocity, grad_lift, grad_taps, grad_point, grad_out = results
    return grad_velocity, grad_lift.T, jnp.transpose(grad_taps, (1, 2, 0)), grad_point, grad_out


def either(velocity, cotangent, lift_weight, depth_kernels, point_weights, out_weight):
    groups_y, groups_x = lax.axis_size("ha"), lax.axis_size("wa")
    layers, channels, _ = depth_kernels.shape
    _, rows, cols = velocity.shape
    per = groups_y * cols // (groups_x * groups_y)
    fits = layers == 1 and channels == 64 and rows == 32 and cols % 256 == 0
    fits = fits and per % 32 == 0 and groups_y * cols <= 1024 and groups_x * rows == 256
    run = fused if fits else local
    return run(velocity, cotangent, lift_weight, depth_kernels, point_weights, out_weight)


def solution(mesh):
    return jax.shard_map(
        either,
        mesh=mesh,
        in_specs=(P(None, "wa", "ha"), P(None, "wa", "ha"), P(), P(), P(), P()),
        out_specs=(P(None, "wa", "ha"), P(), P(), P(), P()),
        check_vma=False,
    )
```

```python
import functools
import math

import jax
import jax.numpy as jnp
import ml_dtypes
import numpy as np
from jax import lax
from jax.experimental import pallas as pl
from jax.experimental.pallas import tpu as pltpu
from jax.sharding import PartitionSpec as P

OFFSETS = ((-1, -1), (-1, 0), (-1, 1), (0, -1), (0, 0), (0, 1), (1, -1), (1, 0), (1, 1))
TWO_PI = 2.0 * math.pi


def extended(value, sides, width):
    for axis, dim in sides:
        size, length = (lax.axis_size(axis), value.shape[dim])
        up = [(i, (i + 1) % size) for i in range(size)]
        down = [(j, i) for i, j in up]
        last = lax.slice_in_dim(value, length - width, length, axis=dim)
        leading = lax.slice_in_dim(value, 0, width, axis=dim)
        before = lax.ppermute(last, axis, up)
        after = lax.ppermute(leading, axis, down)
        value = jnp.concatenate([before, value, after], axis=dim)
    return value


def dft_table(table_len, sign_val):
    ids = jnp.arange(table_len, dtype=jnp.int32)
    product = ids[:, None] * ids[None, :] % table_len
    phase_angle = sign_val * TWO_PI / table_len * product.astype(jnp.float32)
    return (jnp.cos(phase_angle), jnp.sin(phase_angle))


def apply_table(values, tab_real, tab_imag):
    highest = lax.Precision.HIGHEST
    real_part = values[0]
    imag_part = values[1]
    out_real = jnp.einsum("...n,kn->...k", real_part, tab_real, precision=highest) - jnp.einsum(
        "...n,kn->...k", imag_part, tab_imag, precision=highest
    )
    out_imag = jnp.einsum("...n,kn->...k", real_part, tab_imag, precision=highest) + jnp.einsum(
        "...n,kn->...k", imag_part, tab_real, precision=highest
    )
    return jnp.stack([out_real, out_imag])


def rotate(values, phase_angle):
    cosine = jnp.cos(phase_angle)
    sine_val = jnp.sin(phase_angle)
    return jnp.stack(
        [values[0] * cosine - values[1] * sine_val, values[0] * sine_val + values[1] * cosine]
    )


def forward_first(values, axis_dim, groups, own_index, length):
    moved = jnp.moveaxis(values, axis_dim, -1)
    leading = moved.shape[:-1]
    full_len = moved.shape[-1]
    piece_len = full_len // groups
    moved = jnp.swapaxes(moved.reshape(leading + (groups, piece_len)), -1, -2)
    tab_real, tab_imag = dft_table(groups, -1.0)
    moved = apply_table(moved, tab_real, tab_imag)
    local_m = jnp.arange(piece_len, dtype=jnp.int32)[:, None] + own_index * piece_len
    first_k = jnp.arange(groups, dtype=jnp.int32)[None, :]
    phase_angle = -TWO_PI / length * (local_m * first_k % length).astype(jnp.float32)
    moved = rotate(moved, phase_angle)
    moved = jnp.swapaxes(moved, -1, -2).reshape(leading + (full_len,))
    return jnp.moveaxis(moved, -1, axis_dim)


def forward_second(values, axis_dim):
    moved = jnp.moveaxis(values, axis_dim, -1)
    tab_real, tab_imag = dft_table(moved.shape[-1], -1.0)
    moved = apply_table(moved, tab_real, tab_imag)
    return jnp.moveaxis(moved, -1, axis_dim)


def inverse_first(values, axis_dim, own_index, length):
    moved = jnp.moveaxis(values, axis_dim, -1)
    full_len = moved.shape[-1]
    tab_real, tab_imag = dft_table(full_len, 1.0)
    moved = apply_table(moved, tab_real, tab_imag)
    local_m = jnp.arange(full_len, dtype=jnp.int32)
    phase_angle = TWO_PI / length * (local_m * own_index % length).astype(jnp.float32)
    moved = rotate(moved, phase_angle)
    return jnp.moveaxis(moved, -1, axis_dim)


def inverse_second(values, axis_dim, groups):
    moved = jnp.moveaxis(values, axis_dim, -1)
    leading = moved.shape[:-1]
    full_len = moved.shape[-1]
    piece_len = full_len // groups
    moved = jnp.swapaxes(moved.reshape(leading + (groups, piece_len)), -1, -2)
    tab_real, tab_imag = dft_table(groups, 1.0)
    moved = apply_table(moved, tab_real, tab_imag)
    moved = jnp.swapaxes(moved, -1, -2).reshape(leading + (full_len,))
    return jnp.moveaxis(moved, -1, axis_dim)


def signed_waves(own_index, groups, count_n):
    ids = own_index + groups * jnp.arange(count_n, dtype=jnp.int32)
    total_len = groups * count_n
    return jnp.where(2 * ids >= total_len, ids - total_len, ids).astype(jnp.float32)


def project(spectrum, wave_x, wave_y):
    along_k = wave_x * spectrum[:, 0] + wave_y * spectrum[:, 1]
    factor = along_k / jnp.maximum(wave_x * wave_x + wave_y * wave_y, 1.0)
    return jnp.stack([spectrum[:, 0] - wave_x * factor, spectrum[:, 1] - wave_y * factor], axis=1)


def depthwise_valid(padded, kernel):
    rows_in = padded.shape[1] - 2
    cols_in = padded.shape[2] - 2
    total = jnp.zeros((padded.shape[0], rows_in, cols_in), jnp.float32)
    for offset_id in range(9):
        step_x, step_y = OFFSETS[offset_id]
        total = (
            total
            + kernel[:, offset_id][:, None, None]
            * padded[:, 1 + step_x : 1 + step_x + rows_in, 1 + step_y : 1 + step_y + cols_in]
        )
    return total


def transposed_add(grad_hidden, grad_pad, kernel):
    rows_in = grad_hidden.shape[1]
    cols_in = grad_hidden.shape[2]
    for offset_id in range(9):
        step_x, step_y = OFFSETS[offset_id]
        grad_hidden = (
            grad_hidden
            + kernel[:, offset_id][:, None, None]
            * grad_pad[:, 1 - step_x : 1 - step_x + rows_in, 1 - step_y : 1 - step_y + cols_in]
        )
    return grad_hidden


def kernel_grad(grad_depth, padded):
    rows_in = grad_depth.shape[1]
    cols_in = grad_depth.shape[2]
    grad_full = grad_depth.astype(jnp.float32)
    entries = []
    for offset_id in range(9):
        step_x, step_y = OFFSETS[offset_id]
        window = padded[
            :, 1 + step_x : 1 + step_x + rows_in, 1 + step_y : 1 + step_y + cols_in
        ].astype(jnp.float32)
        entries.append(jnp.sum(grad_full * window, axis=(1, 2)))
    return jnp.stack(entries, axis=1)


def local(velocity, cotangent, lift_weight, depth_kernels, point_weights, out_weight):
    highest = lax.Precision.HIGHEST
    layers = depth_kernels.shape[0]
    cols_n = velocity.shape[1]
    rows_n = velocity.shape[2]
    groups_x = lax.axis_size("wa")
    groups_y = lax.axis_size("ha")
    own_x = lax.axis_index("wa")
    own_y = lax.axis_index("ha")
    length_x = cols_n * groups_x
    length_y = rows_n * groups_y
    spectrum = jnp.stack([cotangent, jnp.zeros_like(cotangent)])
    wave_x = signed_waves(own_x, groups_x, cols_n)[:, None]
    wave_y = signed_waves(own_y, groups_y, rows_n)[None, :]

    def move_x(values):
        return lax.all_to_all(values, "wa", split_axis=2, concat_axis=2, tiled=True)

    def move_y(values):
        return lax.all_to_all(values, "ha", split_axis=3, concat_axis=3, tiled=True)

    spectrum = forward_first(move_x(spectrum), 2, groups_x, own_x, length_x)
    spectrum = forward_second(move_x(spectrum), 2)
    spectrum = forward_first(move_y(spectrum), 3, groups_y, own_y, length_y)
    spectrum = forward_second(move_y(spectrum), 3)
    spectrum = project(spectrum, wave_x, wave_y)
    spectrum = move_y(inverse_first(spectrum, 3, own_y, length_y))
    spectrum = move_y(inverse_second(spectrum, 3, groups_y))
    spectrum = move_x(inverse_first(spectrum, 2, own_x, length_x))
    spectrum = move_x(inverse_second(spectrum, 2, groups_x))
    grad_proj = spectrum[0] / float(length_x * length_y)
    saved_pad, saved_depth, saved_tanh = ([], [], [])
    hidden = jnp.einsum("cs,sxy->cxy", lift_weight, velocity, precision=highest).astype(
        jnp.bfloat16
    )
    layer_id = 0
    padded = extended(hidden, (("ha", 2), ("wa", 1)), 1)
    depth_out = depthwise_valid(padded, depth_kernels[layer_id]).astype(jnp.bfloat16)
    mixed_pre = jnp.einsum(
        "oc,cxy->oxy", point_weights[layer_id], depth_out, preferred_element_type=jnp.float32
    )
    squash = jnp.tanh(mixed_pre).astype(jnp.bfloat16)
    saved_pad.append(padded)
    saved_depth.append(depth_out)
    saved_tanh.append(squash)
    hidden = (hidden.astype(jnp.float32) + squash.astype(jnp.float32)).astype(jnp.bfloat16)
    grad_proj_b = grad_proj.astype(jnp.bfloat16)
    out_sum = jnp.einsum("sxy,cxy->sc", grad_proj_b, hidden, preferred_element_type=jnp.float32)
    grad_hidden = jnp.einsum(
        "sc,sxy->cxy", out_weight, grad_proj_b, preferred_element_type=jnp.float32
    )
    kernel_sums = [None] * layers
    point_sums = [None] * layers
    for layer_id in reversed(range(layers)):
        squash_full = saved_tanh[layer_id].astype(jnp.float32)
        grad_mixed = (grad_hidden * (1.0 - squash_full * squash_full)).astype(jnp.bfloat16)
        point_sums[layer_id] = jnp.einsum(
            "oxy,cxy->oc", grad_mixed, saved_depth[layer_id], preferred_element_type=jnp.float32
        )
        grad_depth = jnp.einsum(
            "oc,oxy->cxy", point_weights[layer_id], grad_mixed, preferred_element_type=jnp.float32
        ).astype(jnp.bfloat16)
        grad_pad = extended(grad_depth, (("ha", 2), ("wa", 1)), 1)
        kernel_sums[layer_id] = kernel_grad(grad_depth, saved_pad[layer_id])
        grad_hidden = transposed_add(grad_hidden, grad_pad, depth_kernels[layer_id])
    lift_sum = jnp.einsum("cxy,sxy->cs", grad_hidden, velocity, precision=highest)
    grad_velocity = grad_proj + jnp.einsum(
        "cs,cxy->sxy", lift_weight, grad_hidden, precision=highest
    )
    totals = lax.psum(
        (lift_sum, jnp.stack(kernel_sums), jnp.stack(point_sums), out_sum), ("ha", "wa")
    )
    scale = 1.0 / math.sqrt(length_x * length_y)
    return (
        grad_velocity,
        totals[0] * scale,
        totals[1] * scale,
        totals[2] * scale,
        totals[3] * scale,
    )


def real_basis(pairs, is_sin, positions, length):
    angle = 2.0 * np.pi / length * (np.outer(pairs, positions) % length)
    sines = np.where(pairs[:, None] == 0, np.cos(np.pi * positions)[None, :], np.sin(angle))
    return np.where(is_sin[:, None], sines, np.cos(angle))


def make_tables(groups_y, groups_x, rows, cols):
    length_x, length_y = groups_x * rows, groups_y * cols
    per = length_y // (groups_x * groups_y)
    half = per // 2
    ids = np.arange(length_y)
    pair_y = (ids // per) * half + ids % half
    sin_y = (ids % per) >= half
    forward_y = real_basis(pair_y, sin_y, np.arange(length_y), length_y)
    forward_y = forward_y.reshape(groups_y, cols, length_y)
    lanes = np.arange(cols + 128)
    local_y = np.where(lanes > cols, -1, lanes)
    keep_y = (lanes <= cols) | (lanes == cols + 127)
    inverse_y = np.stack(
        [
            real_basis(pair_y, sin_y, (h * cols + local_y) % length_y, length_y) * keep_y
            for h in range(groups_y)
        ]
    )
    kx = np.arange(length_x)
    pair_x = kx % (length_x // 2)
    sin_x = kx >= length_x // 2
    basis_x = real_basis(pair_x, sin_x, np.arange(length_x), length_x)
    forward_x = np.zeros((groups_x, 2, rows, 2, length_x))
    band = rows + 8
    inverse_x = np.zeros((2, length_x, groups_x, 128))
    local_x = np.arange(band)
    keep_x = (local_x <= rows) | (local_x == band - 1)
    local_x = np.where(local_x > rows, -1, local_x)
    for s in range(2):
        forward_x[:, s, :, s, :] = basis_x.T.reshape(groups_x, rows, length_x)
        for w in range(groups_x):
            part = basis_x[:, (w * rows + local_x) % length_x] * keep_x
            inverse_x[s, :, w, s * band : (s + 1) * band] = part
    forward_x = forward_x.reshape(groups_x, 2 * rows, 2 * length_x)
    inverse_x = inverse_x.reshape(2 * length_x, groups_x * 128)

    def halves(table, axis):
        coarse = table.astype(ml_dtypes.bfloat16)
        fine = (table - coarse.astype(np.float64)).astype(ml_dtypes.bfloat16)
        return np.stack([coarse, fine], axis=axis)

    forward_x = halves(forward_x, 1)
    forward_x = np.concatenate([forward_x[:, 0], forward_x[:, 0], forward_x[:, 1]], axis=1)
    return halves(forward_y, 1), halves(inverse_y, 1), forward_x, halves(inverse_x, 0)


def dot(a, b, dims=((1,), (0,))):
    return lax.dot_general(a, b, (dims, ((), ())), preferred_element_type=jnp.float32)


def put(ref, start, count, stride, value):
    for tile in range(ref.shape[0]):
        ref[tile, pl.ds(start, count, stride=stride), :] = value[:, tile * 128 : (tile + 1) * 128]


def take(ref, start, count, stride=1, tiles=None):
    rows = pl.ds(start, count, stride=stride)
    parts = [ref[tile, rows, :] for tile in range(tiles or ref.shape[0])]
    return jnp.concatenate(parts, axis=1)


def halved(value, axis):
    coarse = value.astype(jnp.bfloat16)
    fine = (value - coarse.astype(jnp.float32)).astype(jnp.bfloat16)
    return jnp.concatenate([coarse, fine], axis=axis)


def widened(lift, taps):
    empty = jnp.zeros((2, lift.shape[1]), jnp.float32)
    lift_wide, taps_wide = [], []
    for a in range(3):
        for k in range(2):
            lift_wide += [lift[k : k + 1]] * 3
            taps_wide += [taps[3 * a : 3 * a + 3]]
        lift_wide.append(empty)
        taps_wide.append(empty)
    return jnp.concatenate(lift_wide, axis=0), jnp.concatenate(taps_wide, axis=0)


def fused_kernel(
    groups_y,
    groups_x,
    rows,
    cols,
    vel_hbm,
    cot_hbm,
    lift_hbm,
    taps_hbm,
    point_hbm,
    outw_hbm,
    fy_hbm,
    iy_hbm,
    fx_hbm,
    ix_hbm,
    gv_hbm,
    sums_hbm,
    gv_ref,
    sums_ref,
    vel_ref,
    cot_ref,
    lift_ref,
    taps_ref,
    point_ref,
    outw_ref,
    fy,
    iy,
    fx,
    ix,
    gath,
    send2,
    recv2,
    send3,
    recv3,
    gath4,
    halo_out,
    halo_in,
    edge_out,
    edge_in,
    ext,
    shifts,
    tbuf,
    slope,
    gp2,
    ubuf,
    pay_y,
    pay_x,
    table_sem,
    s1,
    r1,
    s2,
    r2,
    s3,
    r3,
    s4,
    r4,
    sh,
    rh,
    se,
    re,
    s5,
    r5,
    s6,
    r6,
):
    bf16, f32 = jnp.bfloat16, jnp.float32
    h = lax.axis_index("ha")
    w = lax.axis_index("wa")
    length_x, length_y = groups_x * rows, groups_y * cols
    per = length_y // (groups_x * groups_y)
    half = per // 2
    wide = cols + 128
    band = rows + 8

    loads = [
        pltpu.make_async_copy(fy_hbm.at[h], fy, table_sem.at[0]),
        pltpu.make_async_copy(iy_hbm.at[h], iy, table_sem.at[1]),
        pltpu.make_async_copy(fx_hbm, fx, table_sem.at[2]),
        pltpu.make_async_copy(ix_hbm, ix, table_sem.at[3]),
    ]
    pairs = [
        (cot_hbm, cot_ref),
        (vel_hbm, vel_ref),
        (lift_hbm, lift_ref),
        (taps_hbm, taps_ref),
        (point_hbm, point_ref),
        (outw_hbm, outw_ref),
    ]
    small = [
        pltpu.make_async_copy(src, dst, table_sem.at[4 + i]) for i, (src, dst) in enumerate(pairs)
    ]
    for load in small + [loads[0], loads[2], loads[3], loads[1]]:
        load.start()

    def ha_peer(step):
        return lax.rem(h + step, groups_y)

    def wa_peer(step):
        return lax.rem(w + step, groups_x)

    barrier = pltpu.get_barrier_semaphore()
    for step in range(1, groups_y):
        pl.semaphore_signal(
            barrier, inc=1, device_id=(ha_peer(step), w), device_id_type=pl.DeviceIdType.MESH
        )
    for step in range(1, groups_x):
        pl.semaphore_signal(
            barrier, inc=1, device_id=(h, wa_peer(step)), device_id_type=pl.DeviceIdType.MESH
        )

    def remote(src, dst, send, recv, device):
        return pltpu.make_async_remote_copy(
            src_ref=src,
            dst_ref=dst,
            send_sem=send,
            recv_sem=recv,
            device_id=device,
            device_id_type=pl.DeviceIdType.MESH,
        )

    small[0].wait()
    gath[h] = halved(cot_ref[...].reshape(2 * rows, cols), 0)
    small[1].wait()
    vel = vel_ref[...].reshape(2 * rows, cols)
    halo_out[0] = vel[:, :128]
    halo_out[1] = vel[:, cols - 128 :]
    pl.semaphore_wait(barrier, groups_y + groups_x - 2)

    def spread_y(buf, send, recv):
        copies = []
        for step in range(1, groups_y):
            copy = remote(buf.at[h], buf.at[h], send.at[step], recv.at[h], (ha_peer(step), w))
            copy.start()
            copies.append(copy)
        return copies

    def arrived_y(buf, send, recv, step):
        src = ha_peer(step)
        remote(buf.at[src], buf.at[src], send.at[step], recv.at[src], (src, w)).wait_recv()
        return src

    def spread_x(src_of, buf, send, recv):
        copies = []
        for step in range(1, groups_x):
            dst = wa_peer(step)
            copy = remote(src_of(dst), buf.at[w], send.at[step], recv.at[w], (h, dst))
            copy.start()
            copies.append(copy)
        return copies

    def arrived_x(buf, send, recv, step):
        src = wa_peer(step)
        remote(buf.at[src], buf.at[src], send.at[step], recv.at[src], (h, src)).wait_recv()
        return src

    pending = spread_y(gath, s1, r1)
    left, right = (ha_peer(groups_y - 1), w), (ha_peer(1), w)
    halo = [
        remote(halo_out.at[0], halo_in.at[0], sh.at[0], rh.at[0], left),
        remote(halo_out.at[1], halo_in.at[1], sh.at[1], rh.at[1], right),
    ]
    for copy in halo:
        copy.start()

    for load in small[2:]:
        load.wait()
    lift = lift_ref[...]
    taps = taps_ref[:, 0, :]
    point = point_ref[0]
    outw = outw_ref[...].astype(f32)
    lift_wide, taps_wide = widened(lift, taps)
    both = lift_wide * taps_wide
    mixed = dot(halved(both, 0), point, ((1,), (1,)))
    mixed = mixed[:24] + mixed[24:]
    coarse = mixed.astype(bf16).astype(f32)
    stack = [coarse, mixed - coarse, coarse, jnp.zeros((56, 64), f32)]
    stack = jnp.pad(jnp.concatenate(stack, axis=0), ((0, 0), (0, 64)))
    mixed_b = jnp.transpose(stack)[:64, :80].astype(bf16)
    none = jnp.zeros((8, wide), f32)
    out_pad = jnp.concatenate([outw, jnp.zeros((14, 64), f32)], axis=0)
    columns = jnp.transpose(jnp.pad(out_pad, ((0, 112), (0, 64))))
    out_0 = jnp.broadcast_to(columns[:64, 0:1], (64, wide))
    out_1 = jnp.broadcast_to(columns[:64, 1:2], (64, wide))
    lift_pad = jnp.concatenate([lift, jnp.zeros((6, 64), f32)], axis=0)
    through = dot(halved(lift_pad, 0), out_pad.astype(bf16), ((1,), (1,)))
    through = through[:8] + through[8:]
    row_24 = lax.broadcasted_iota(jnp.int32, (24, 16), 0)
    place = jnp.where(row_24 == 9, through[0:1], jnp.where(row_24 == 12, through[1:2], 0.0))
    back_b = jnp.concatenate([mixed, place], axis=1).astype(bf16)

    row_id = lax.broadcasted_iota(jnp.int32, (per, length_x), 0)
    lane_id = lax.broadcasted_iota(jnp.int32, (per, length_x), 1)
    py = (h * groups_x + w) * half + lax.rem(row_id, half)
    px = lax.rem(lane_id, length_x // 2)
    ysin, xsin = row_id >= half, lane_id >= length_x // 2
    ky = jnp.where((py == 0) & ysin, length_y // 2, py).astype(f32)
    kx = jnp.where((px == 0) & xsin, length_x // 2, px).astype(f32)
    weight = jnp.where(py == 0, 1.0, 2.0) * jnp.where(px == 0, 1.0, 2.0) / (length_x * length_y)
    inverse_k = weight / jnp.maximum(kx * kx + ky * ky, 1.0)
    keep_0 = weight - kx * kx * inverse_k
    keep_1 = weight - ky * ky * inverse_k
    cross = kx * ky * inverse_k
    inner = (px != 0) & (py != 0)
    turn = jnp.where(inner, jnp.where(ysin == xsin, -cross, cross), 0.0)
    corner = jnp.where((px == 0) & (py == 0) & ysin & xsin, cross, 0.0)

    loads[0].wait()
    spec = jnp.zeros((cols, 2 * rows), f32)
    for step in range(groups_y):
        src = h if step == 0 else arrived_y(gath, s1, r1, step)
        where = pl.ds(pl.multiple_of(src * cols, cols), cols)
        field = gath[src]
        both_parts = dot(fy[0, :, where], field, ((1,), (1,)))
        spec = spec + both_parts[:, : 2 * rows] + both_parts[:, 2 * rows :]
        spec = spec + dot(fy[1, :, where], field[: 2 * rows], ((1,), (1,)))
    send2[...] = halved(spec, 1).reshape(groups_x, per, 4 * rows)
    pending += spread_x(lambda dst: send2.at[dst], recv2, s2, r2)
    recv2[w] = send2[w]

    for copy in halo:
        copy.wait()
    side = lax.broadcasted_iota(jnp.int32, (2 * rows, 128), 1)
    tail = jnp.where(side < 64, halo_in[0], halo_in[1])
    ext[:, :cols] = vel
    ext[:, cols:] = tail
    edge_out[...] = jnp.zeros_like(edge_out)
    for s in range(2):
        edge_out[0, 2 * s : 2 * s + 2, :] = ext[s * rows : s * rows + 2, :]
        edge_out[1, 2 * s : 2 * s + 2, :] = ext[s * rows + rows - 2 : s * rows + rows, :]
    edges = [
        remote(edge_out.at[0], edge_in.at[0], se.at[0], re.at[0], (h, wa_peer(groups_x - 1))),
        remote(edge_out.at[1], edge_in.at[1], se.at[1], re.at[1], (h, wa_peer(1))),
    ]
    for copy in edges:
        copy.start()
    shifts[...] = jnp.zeros_like(shifts)
    for s in range(2):
        for b in range(3):
            moved = ext[s * rows : (s + 1) * rows, :]
            if b != 1:
                moved = pltpu.roll(moved, (1 - b) % wide, 1)
            put(shifts, 16 + s * 3 + b, rows, 8, moved)

    def forward_row(n):
        start = n * 8 if isinstance(n, int) else pl.multiple_of(8 * n, 8)
        window = take(shifts, start, 24)
        coarse = window.astype(bf16).astype(f32)
        window = jnp.concatenate([coarse, coarse, window - coarse, none], axis=0)
        tan = jnp.tanh(dot(mixed_b, window.astype(bf16)))
        tbuf[n] = tan.astype(bf16)
        slope[n] = (1.0 - tan * tan).astype(bf16)

    def forward_rows(first, count):
        def two(i, carry):
            forward_row(first + 2 * i)
            forward_row(first + 2 * i + 1)
            return carry

        lax.fori_loop(0, count // 2, two, 0)

    forward_rows(2, 4)

    loads[2].wait()
    waves = jnp.zeros((per, 2 * length_x), f32)
    for step in range(groups_x):
        src = w if step == 0 else arrived_x(recv2, s2, r2, step)
        got = recv2[src]
        waves = waves + dot(jnp.concatenate([got, got[:, : 2 * rows]], axis=1), fx[src])
    a0, a1 = waves[:, :length_x], waves[:, length_x:]

    def swapped(a):
        a = jnp.concatenate([a[half:], a[:half]], axis=0)
        return jnp.concatenate([a[:, length_x // 2 :], a[:, : length_x // 2]], axis=1)

    p0 = keep_0 * a0 - turn * swapped(a1) - corner * a1
    p1 = keep_1 * a1 - turn * swapped(a0) - corner * a0
    loads[3].wait()
    split = halved(jnp.concatenate([p0, p1], axis=1), 0)
    fields = dot(split, ix[0])
    fields = (fields[:per] + fields[per:] + dot(split[:per], ix[1])).astype(bf16)
    for dst in range(groups_x):
        send3[dst] = fields[:, dst * 128 : (dst + 1) * 128]
    pending += spread_x(lambda dst: send3.at[dst], recv3, s3, r3)
    recv3[w] = send3[w]

    forward_rows(6, 10)
    for copy in edges:
        copy.wait()
    for s in range(2):
        for b in range(3):
            for slot, first in ((1, 0), (0, rows + 2)):
                moved = edge_in[slot]
                if b != 1:
                    moved = pltpu.roll(moved, (1 - b) % wide, 1)
                for i in range(2):
                    at = 8 * (first + i) + s * 3 + b
                    put(shifts, at, 1, 1, moved[2 * s + i : 2 * s + i + 1])

    for step in range(1, groups_x):
        arrived_x(recv3, s3, r3, step)
    turned = jnp.transpose(recv3[...].reshape(cols, 128).astype(f32))
    gath4[h] = turned[: 2 * band].astype(bf16)
    pending += spread_y(gath4, s4, r4)

    forward_rows(16, rows - 16)
    for n in (0, 1, rows, rows + 1):
        forward_row(n)
    loads[1].wait()
    field = jnp.zeros((2 * band, wide), f32)
    for step in range(groups_y):
        src = h if step == 0 else arrived_y(gath4, s4, r4, step)
        where = pl.ds(pl.multiple_of(src * cols, cols), cols)
        got = gath4[src]
        field = field + dot(got, iy[0, where, :]) + dot(got, iy[1, where, :])
    gp2[...] = jnp.zeros_like(gp2)
    for s in range(2):
        part = field[s * band : (s + 1) * band]
        put(gp2, 8 + s, rows, 8, part[:rows])
        put(gp2, 8 * (rows + 1) + s, 1, 1, part[rows : rows + 1])
        put(gp2, s, 1, 1, part[band - 1 :])

    def backward_row(n, own):
        gp8 = take(gp2, pl.multiple_of(8 * n, 8), 8)
        gp16 = jnp.concatenate([gp8, jnp.zeros_like(gp8)], axis=0).astype(bf16)
        tan = tbuf[n]
        gpb = gp16.astype(f32)
        grad = out_0 * gpb[0:1] + out_1 * gpb[1:2]
        gz = (grad * slope[n].astype(f32)).astype(bf16)
        back = dot(back_b, jnp.concatenate([gz, gp16], axis=0))
        put(ubuf, pl.multiple_of(24 * n, 8), 24, 1, back)
        if not own:
            return None
        window = take(shifts, pl.multiple_of(8 * n, 8), 24, tiles=cols // 128)
        coarse = window.astype(bf16).astype(f32)
        pad = jnp.zeros_like(gp8[:, :cols])
        right_side = [window, gp8[:, :cols], window - coarse, pad]
        right_side = jnp.concatenate(right_side, axis=0).astype(bf16)
        left_side = jnp.concatenate([gz[:, :cols], tan[:, :cols], gp16[:, :cols]], axis=0)
        return dot(left_side, right_side, ((1,), (1,)))

    def backward_rows(i, total):
        for j in range(4):
            total = total + backward_row(1 + 4 * i + j, True)
        return total

    acc = lax.fori_loop(0, rows // 4, backward_rows, jnp.zeros((144, 64), f32))
    acc = acc[:, :32] + acc[:, 32:]

    low = lax.broadcasted_iota(jnp.int32, (64, 32), 1) < 24
    packed = jnp.concatenate(
        [jnp.where(low, acc[:64], acc[64:128]), acc[128:144], jnp.zeros((48, 32), f32)], axis=0
    )
    packed = jnp.transpose(jnp.pad(packed, ((0, 0), (0, 96))))[:32]
    upper = [packed[16:26, :64], packed[9:10, 64:], packed[12:13, 64:], packed[28:32, :64]]
    upper = jnp.concatenate(upper, axis=0)
    pay_y[h] = jnp.concatenate([packed[:16, :64], upper], axis=1)
    pending += spread_y(pay_y, s5, r5)

    backward_row(0, False)
    backward_row(rows + 1, False)
    for s in range(2):
        result = take(gp2, 8 + s, rows, 8)
        for b in range(3):
            k = s * 3 + b
            part = (
                take(ubuf, 48 + k, rows, 24)
                + take(ubuf, 24 + 8 + k, rows, 24)
                + take(ubuf, 16 + k, rows, 24)
            )
            if b != 1:
                part = pltpu.roll(part, (b - 1) % wide, 1)
            result = result + part
        gv_ref[s] = result[:, :cols]
    leave_gv = pltpu.make_async_copy(gv_ref, gv_hbm, table_sem.at[10])
    leave_gv.start()

    for step in range(1, groups_y):
        arrived_y(pay_y, s5, r5, step)
    summed = pay_y[0]
    for src in range(1, groups_y):
        summed = summed + pay_y[src]
    pay_x[w] = summed
    pending += spread_x(lambda dst: pay_x.at[w], pay_x, s6, r6)
    for step in range(1, groups_x):
        arrived_x(pay_x, s6, r6, step)
    sums = pay_x[0]
    for src in range(1, groups_x):
        sums = sums + pay_x[src]
    sums = sums * (1.0 / math.sqrt(length_x * length_y))
    sums_ref[...] = sums
    leave = pltpu.make_async_copy(sums_ref, sums_hbm, table_sem.at[11])
    leave.start()
    for copy in pending:
        copy.wait_send()
    leave_gv.wait()
    leave.wait()


def finish_kernel(
    gv_in,
    sums_hbm,
    lift_hbm,
    taps_hbm,
    point_hbm,
    outw_hbm,
    gv_out,
    lift_out,
    taps_out,
    point_out,
    out_out,
    sums_ref,
    lift_ref,
    taps_ref,
    point_ref,
    outw_ref,
    glift_ref,
    gtaps_ref,
    gpoint_ref,
    gout_ref,
    sem,
):
    bf16, f32 = jnp.bfloat16, jnp.float32
    pairs = [
        (sums_hbm, sums_ref),
        (lift_hbm, lift_ref),
        (taps_hbm, taps_ref),
        (point_hbm, point_ref),
        (outw_hbm, outw_ref),
    ]
    loads = [pltpu.make_async_copy(a, b, sem.at[i]) for i, (a, b) in enumerate(pairs)]
    pairs = [
        (gv_in, gv_out),
        (glift_ref, lift_out),
        (gtaps_ref, taps_out),
        (gpoint_ref, point_out),
        (gout_ref, out_out),
    ]
    stores = [pltpu.make_async_copy(a, b, sem.at[5 + i]) for i, (a, b) in enumerate(pairs)]
    for load in loads:
        load.start()
    stores[0].start()
    for load in loads:
        load.wait()
    sums = sums_ref[...]
    lift = lift_ref[...]
    point = point_ref[0]
    outw = outw_ref[...].astype(f32)
    lift_wide, taps_wide = widened(lift, taps_ref[:, 0, :])
    both = lift_wide * taps_wide
    gz_sum = jnp.concatenate([sums[:, :64], sums[:8, 64:]], axis=0)
    depth = dot(halved(gz_sum, 0), point)
    depth = depth[:24] + depth[24:]
    fine = gz_sum - gz_sum.astype(bf16).astype(f32)
    left_side = jnp.concatenate([gz_sum, fine, gz_sum, jnp.zeros((56, 64), f32)], axis=0)
    left_side = jnp.transpose(jnp.pad(left_side, ((0, 0), (0, 64))))[:64, :80].astype(bf16)
    fine = both - both.astype(bf16).astype(f32)
    right_side = jnp.concatenate([both, both, fine, jnp.zeros((8, 64), f32)], axis=0).astype(bf16)
    gpoint_ref[0] = dot(left_side, right_side)
    by_tap = depth * lift_wide
    by_lift = depth * taps_wide
    for a in range(3):
        for b in range(3):
            k = 8 * a + b
            gtaps_ref[3 * a + b] = by_tap[k : k + 1] + by_tap[k + 3 : k + 4]
    for s in range(2):
        total = jnp.zeros((1, 64), f32)
        for a in range(3):
            k = 8 * a + 3 * s
            total = total + jnp.sum(by_lift[k : k + 3], axis=0, keepdims=True)
        for r in range(2):
            total = total + sums[10 + s : 11 + s, 64 + r : 65 + r] * outw[r : r + 1]
        glift_ref[s : s + 1] = total
        total = sums[8 + s : 9 + s, 64:]
        for r in range(2):
            total = total + sums[10 + r : 11 + r, 64 + s : 65 + s] * lift[r : r + 1]
        gout_ref[s : s + 1] = total
    for store in stores[1:]:
        store.start()
    for store in stores:
        store.wait()


def fused(velocity, cotangent, lift_weight, depth_kernels, point_weights, out_weight):
    groups_y, groups_x = lax.axis_size("ha"), lax.axis_size("wa")
    _, rows, cols = velocity.shape
    channels = lift_weight.shape[0]
    length_x, length_y = groups_x * rows, groups_y * cols
    per = length_y // (groups_x * groups_y)
    wide = cols + 128
    tables = make_tables(groups_y, groups_x, rows, cols)
    bf16, f32 = jnp.bfloat16, jnp.float32
    dma = pltpu.SemaphoreType.DMA
    hbm = pl.BlockSpec(memory_space=pltpu.HBM)
    lift_t = lift_weight.T
    taps_t = jnp.transpose(depth_kernels, (2, 0, 1))
    grad_velocity, sums = pl.pallas_call(
        functools.partial(fused_kernel, groups_y, groups_x, rows, cols),
        out_shape=(
            jax.ShapeDtypeStruct((2, rows, cols), f32),
            jax.ShapeDtypeStruct((16, 128), f32),
        ),
        in_specs=[hbm] * 10,
        out_specs=(hbm, hbm),
        scratch_shapes=[
            pltpu.VMEM((2, rows, cols), f32),
            pltpu.VMEM((16, 128), f32),
            pltpu.VMEM((2, rows, cols), f32),
            pltpu.VMEM((2, rows, cols), f32),
            pltpu.VMEM((2, channels), f32),
            pltpu.VMEM((9, 1, channels), f32),
            pltpu.VMEM((1, channels, channels), bf16),
            pltpu.VMEM((2, channels), bf16),
            pltpu.VMEM((2, cols, length_y), bf16),
            pltpu.VMEM((2, length_y, wide), bf16),
            pltpu.VMEM((groups_x, 6 * rows, 2 * length_x), bf16),
            pltpu.VMEM((2, 2 * length_x, groups_x * 128), bf16),
            pltpu.VMEM((groups_y, 4 * rows, cols), bf16),
            pltpu.VMEM((groups_x, per, 4 * rows), bf16),
            pltpu.VMEM((groups_x, per, 4 * rows), bf16),
            pltpu.VMEM((groups_x, per, 128), bf16),
            pltpu.VMEM((groups_x, per, 128), bf16),
            pltpu.VMEM((groups_y, 2 * (rows + 8), cols), bf16),
            pltpu.VMEM((2, 2 * rows, 128), f32),
            pltpu.VMEM((2, 2 * rows, 128), f32),
            pltpu.VMEM((2, 8, wide), f32),
            pltpu.VMEM((2, 8, wide), f32),
            pltpu.VMEM((2 * rows, wide), f32),
            pltpu.VMEM((wide // 128, 8 * (rows + 4), 128), f32),
            pltpu.VMEM((rows + 2, channels, wide), bf16),
            pltpu.VMEM((rows + 2, channels, wide), bf16),
            pltpu.VMEM((wide // 128, 8 * (rows + 2), 128), f32),
            pltpu.VMEM((wide // 128, 24 * (rows + 2), 128), f32),
            pltpu.VMEM((groups_y, 16, 128), f32),
            pltpu.VMEM((groups_x, 16, 128), f32),
            dma((12,)),
            dma((groups_y,)),
            dma((groups_y,)),
            dma((groups_x,)),
            dma((groups_x,)),
            dma((groups_x,)),
            dma((groups_x,)),
            dma((groups_y,)),
            dma((groups_y,)),
            dma((2,)),
            dma((2,)),
            dma((2,)),
            dma((2,)),
            dma((groups_y,)),
            dma((groups_y,)),
            dma((groups_x,)),
            dma((groups_x,)),
        ],
        compiler_params=pltpu.CompilerParams(
            collective_id=0, has_side_effects=True, vmem_limit_bytes=64 * 1024 * 1024
        ),
    )(
        velocity,
        cotangent,
        lift_t,
        taps_t,
        point_weights,
        out_weight,
        *[jnp.asarray(t) for t in tables],
    )
    results = pl.pallas_call(
        finish_kernel,
        out_shape=(
            jax.ShapeDtypeStruct((2, rows, cols), f32),
            jax.ShapeDtypeStruct((2, channels), f32),
            jax.ShapeDtypeStruct((9, 1, channels), f32),
            jax.ShapeDtypeStruct((1, channels, channels), f32),
            jax.ShapeDtypeStruct((2, channels), f32),
        ),
        in_specs=[hbm] * 6,
        out_specs=(hbm,) * 5,
        scratch_shapes=[
            pltpu.VMEM((16, 128), f32),
            pltpu.VMEM((2, channels), f32),
            pltpu.VMEM((9, 1, channels), f32),
            pltpu.VMEM((1, channels, channels), bf16),
            pltpu.VMEM((2, channels), bf16),
            pltpu.VMEM((2, channels), f32),
            pltpu.VMEM((9, 1, channels), f32),
            pltpu.VMEM((1, channels, channels), f32),
            pltpu.VMEM((2, channels), f32),
            dma((10,)),
        ],
        compiler_params=pltpu.CompilerParams(vmem_limit_bytes=64 * 1024 * 1024),
    )(grad_velocity, sums, lift_t, taps_t, point_weights, out_weight)
    grad_velocity, grad_lift, grad_taps, grad_point, grad_out = results
    return grad_velocity, grad_lift.T, jnp.transpose(grad_taps, (1, 2, 0)), grad_point, grad_out


def either(velocity, cotangent, lift_weight, depth_kernels, point_weights, out_weight):
    groups_y, groups_x = lax.axis_size("ha"), lax.axis_size("wa")
    layers, channels, _ = depth_kernels.shape
    _, rows, cols = velocity.shape
    per = groups_y * cols // (groups_x * groups_y)
    fits = layers == 1 and channels == 64 and rows == 32 and cols % 256 == 0
    fits = fits and per % 32 == 0 and groups_y * cols <= 1024 and groups_x * rows == 256
    run = fused if fits else local
    return run(velocity, cotangent, lift_weight, depth_kernels, point_weights, out_weight)


def solution(mesh):
    return jax.shard_map(
        either,
        mesh=mesh,
        in_specs=(P(None, "wa", "ha"), P(None, "wa", "ha"), P(), P(), P(), P()),
        out_specs=(P(None, "wa", "ha"), P(), P(), P(), P()),
        check_vma=False,
    )
```

```python
import functools
import math

import jax
import jax.numpy as jnp
import ml_dtypes
import numpy as np
from jax import lax
from jax.experimental import pallas as pl
from jax.experimental.pallas import tpu as pltpu
from jax.sharding import PartitionSpec as P

OFFSETS = ((-1, -1), (-1, 0), (-1, 1), (0, -1), (0, 0), (0, 1), (1, -1), (1, 0), (1, 1))
TWO_PI = 2.0 * math.pi


def extended(value, sides, width):
    for axis, dim in sides:
        size, length = (lax.axis_size(axis), value.shape[dim])
        up = [(i, (i + 1) % size) for i in range(size)]
        down = [(j, i) for i, j in up]
        last = lax.slice_in_dim(value, length - width, length, axis=dim)
        leading = lax.slice_in_dim(value, 0, width, axis=dim)
        before = lax.ppermute(last, axis, up)
        after = lax.ppermute(leading, axis, down)
        value = jnp.concatenate([before, value, after], axis=dim)
    return value


def dft_table(table_len, sign_val):
    ids = jnp.arange(table_len, dtype=jnp.int32)
    product = ids[:, None] * ids[None, :] % table_len
    phase_angle = sign_val * TWO_PI / table_len * product.astype(jnp.float32)
    return (jnp.cos(phase_angle), jnp.sin(phase_angle))


def apply_table(values, tab_real, tab_imag):
    highest = lax.Precision.HIGHEST
    real_part = values[0]
    imag_part = values[1]
    out_real = jnp.einsum("...n,kn->...k", real_part, tab_real, precision=highest) - jnp.einsum(
        "...n,kn->...k", imag_part, tab_imag, precision=highest
    )
    out_imag = jnp.einsum("...n,kn->...k", real_part, tab_imag, precision=highest) + jnp.einsum(
        "...n,kn->...k", imag_part, tab_real, precision=highest
    )
    return jnp.stack([out_real, out_imag])


def rotate(values, phase_angle):
    cosine = jnp.cos(phase_angle)
    sine_val = jnp.sin(phase_angle)
    return jnp.stack(
        [values[0] * cosine - values[1] * sine_val, values[0] * sine_val + values[1] * cosine]
    )


def forward_first(values, axis_dim, groups, own_index, length):
    moved = jnp.moveaxis(values, axis_dim, -1)
    leading = moved.shape[:-1]
    full_len = moved.shape[-1]
    piece_len = full_len // groups
    moved = jnp.swapaxes(moved.reshape(leading + (groups, piece_len)), -1, -2)
    tab_real, tab_imag = dft_table(groups, -1.0)
    moved = apply_table(moved, tab_real, tab_imag)
    local_m = jnp.arange(piece_len, dtype=jnp.int32)[:, None] + own_index * piece_len
    first_k = jnp.arange(groups, dtype=jnp.int32)[None, :]
    phase_angle = -TWO_PI / length * (local_m * first_k % length).astype(jnp.float32)
    moved = rotate(moved, phase_angle)
    moved = jnp.swapaxes(moved, -1, -2).reshape(leading + (full_len,))
    return jnp.moveaxis(moved, -1, axis_dim)


def forward_second(values, axis_dim):
    moved = jnp.moveaxis(values, axis_dim, -1)
    tab_real, tab_imag = dft_table(moved.shape[-1], -1.0)
    moved = apply_table(moved, tab_real, tab_imag)
    return jnp.moveaxis(moved, -1, axis_dim)


def inverse_first(values, axis_dim, own_index, length):
    moved = jnp.moveaxis(values, axis_dim, -1)
    full_len = moved.shape[-1]
    tab_real, tab_imag = dft_table(full_len, 1.0)
    moved = apply_table(moved, tab_real, tab_imag)
    local_m = jnp.arange(full_len, dtype=jnp.int32)
    phase_angle = TWO_PI / length * (local_m * own_index % length).astype(jnp.float32)
    moved = rotate(moved, phase_angle)
    return jnp.moveaxis(moved, -1, axis_dim)


def inverse_second(values, axis_dim, groups):
    moved = jnp.moveaxis(values, axis_dim, -1)
    leading = moved.shape[:-1]
    full_len = moved.shape[-1]
    piece_len = full_len // groups
    moved = jnp.swapaxes(moved.reshape(leading + (groups, piece_len)), -1, -2)
    tab_real, tab_imag = dft_table(groups, 1.0)
    moved = apply_table(moved, tab_real, tab_imag)
    moved = jnp.swapaxes(moved, -1, -2).reshape(leading + (full_len,))
    return jnp.moveaxis(moved, -1, axis_dim)


def signed_waves(own_index, groups, count_n):
    ids = own_index + groups * jnp.arange(count_n, dtype=jnp.int32)
    total_len = groups * count_n
    return jnp.where(2 * ids >= total_len, ids - total_len, ids).astype(jnp.float32)


def project(spectrum, wave_x, wave_y):
    along_k = wave_x * spectrum[:, 0] + wave_y * spectrum[:, 1]
    factor = along_k / jnp.maximum(wave_x * wave_x + wave_y * wave_y, 1.0)
    return jnp.stack([spectrum[:, 0] - wave_x * factor, spectrum[:, 1] - wave_y * factor], axis=1)


def depthwise_valid(padded, kernel):
    rows_in = padded.shape[1] - 2
    cols_in = padded.shape[2] - 2
    total = jnp.zeros((padded.shape[0], rows_in, cols_in), jnp.float32)
    for offset_id in range(9):
        step_x, step_y = OFFSETS[offset_id]
        total = (
            total
            + kernel[:, offset_id][:, None, None]
            * padded[:, 1 + step_x : 1 + step_x + rows_in, 1 + step_y : 1 + step_y + cols_in]
        )
    return total


def transposed_add(grad_hidden, grad_pad, kernel):
    rows_in = grad_hidden.shape[1]
    cols_in = grad_hidden.shape[2]
    for offset_id in range(9):
        step_x, step_y = OFFSETS[offset_id]
        grad_hidden = (
            grad_hidden
            + kernel[:, offset_id][:, None, None]
            * grad_pad[:, 1 - step_x : 1 - step_x + rows_in, 1 - step_y : 1 - step_y + cols_in]
        )
    return grad_hidden


def kernel_grad(grad_depth, padded):
    rows_in = grad_depth.shape[1]
    cols_in = grad_depth.shape[2]
    grad_full = grad_depth.astype(jnp.float32)
    entries = []
    for offset_id in range(9):
        step_x, step_y = OFFSETS[offset_id]
        window = padded[
            :, 1 + step_x : 1 + step_x + rows_in, 1 + step_y : 1 + step_y + cols_in
        ].astype(jnp.float32)
        entries.append(jnp.sum(grad_full * window, axis=(1, 2)))
    return jnp.stack(entries, axis=1)


def local(velocity, cotangent, lift_weight, depth_kernels, point_weights, out_weight):
    highest = lax.Precision.HIGHEST
    layers = depth_kernels.shape[0]
    cols_n = velocity.shape[1]
    rows_n = velocity.shape[2]
    groups_x = lax.axis_size("wa")
    groups_y = lax.axis_size("ha")
    own_x = lax.axis_index("wa")
    own_y = lax.axis_index("ha")
    length_x = cols_n * groups_x
    length_y = rows_n * groups_y
    spectrum = jnp.stack([cotangent, jnp.zeros_like(cotangent)])
    wave_x = signed_waves(own_x, groups_x, cols_n)[:, None]
    wave_y = signed_waves(own_y, groups_y, rows_n)[None, :]

    def move_x(values):
        return lax.all_to_all(values, "wa", split_axis=2, concat_axis=2, tiled=True)

    def move_y(values):
        return lax.all_to_all(values, "ha", split_axis=3, concat_axis=3, tiled=True)

    spectrum = forward_first(move_x(spectrum), 2, groups_x, own_x, length_x)
    spectrum = forward_second(move_x(spectrum), 2)
    spectrum = forward_first(move_y(spectrum), 3, groups_y, own_y, length_y)
    spectrum = forward_second(move_y(spectrum), 3)
    spectrum = project(spectrum, wave_x, wave_y)
    spectrum = move_y(inverse_first(spectrum, 3, own_y, length_y))
    spectrum = move_y(inverse_second(spectrum, 3, groups_y))
    spectrum = move_x(inverse_first(spectrum, 2, own_x, length_x))
    spectrum = move_x(inverse_second(spectrum, 2, groups_x))
    grad_proj = spectrum[0] / float(length_x * length_y)
    saved_pad, saved_depth, saved_tanh = ([], [], [])
    hidden = jnp.einsum("cs,sxy->cxy", lift_weight, velocity, precision=highest).astype(
        jnp.bfloat16
    )
    layer_id = 0
    padded = extended(hidden, (("ha", 2), ("wa", 1)), 1)
    depth_out = depthwise_valid(padded, depth_kernels[layer_id]).astype(jnp.bfloat16)
    mixed_pre = jnp.einsum(
        "oc,cxy->oxy", point_weights[layer_id], depth_out, preferred_element_type=jnp.float32
    )
    squash = jnp.tanh(mixed_pre).astype(jnp.bfloat16)
    saved_pad.append(padded)
    saved_depth.append(depth_out)
    saved_tanh.append(squash)
    hidden = (hidden.astype(jnp.float32) + squash.astype(jnp.float32)).astype(jnp.bfloat16)
    grad_proj_b = grad_proj.astype(jnp.bfloat16)
    out_sum = jnp.einsum("sxy,cxy->sc", grad_proj_b, hidden, preferred_element_type=jnp.float32)
    grad_hidden = jnp.einsum(
        "sc,sxy->cxy", out_weight, grad_proj_b, preferred_element_type=jnp.float32
    )
    kernel_sums = [None] * layers
    point_sums = [None] * layers
    for layer_id in reversed(range(layers)):
        squash_full = saved_tanh[layer_id].astype(jnp.float32)
        grad_mixed = (grad_hidden * (1.0 - squash_full * squash_full)).astype(jnp.bfloat16)
        point_sums[layer_id] = jnp.einsum(
            "oxy,cxy->oc", grad_mixed, saved_depth[layer_id], preferred_element_type=jnp.float32
        )
        grad_depth = jnp.einsum(
            "oc,oxy->cxy", point_weights[layer_id], grad_mixed, preferred_element_type=jnp.float32
        ).astype(jnp.bfloat16)
        grad_pad = extended(grad_depth, (("ha", 2), ("wa", 1)), 1)
        kernel_sums[layer_id] = kernel_grad(grad_depth, saved_pad[layer_id])
        grad_hidden = transposed_add(grad_hidden, grad_pad, depth_kernels[layer_id])
    lift_sum = jnp.einsum("cxy,sxy->cs", grad_hidden, velocity, precision=highest)
    grad_velocity = grad_proj + jnp.einsum(
        "cs,cxy->sxy", lift_weight, grad_hidden, precision=highest
    )
    totals = lax.psum(
        (lift_sum, jnp.stack(kernel_sums), jnp.stack(point_sums), out_sum), ("ha", "wa")
    )
    scale = 1.0 / math.sqrt(length_x * length_y)
    return (
        grad_velocity,
        totals[0] * scale,
        totals[1] * scale,
        totals[2] * scale,
        totals[3] * scale,
    )


def real_basis(pairs, is_sin, positions, length):
    angle = 2.0 * np.pi / length * (np.outer(pairs, positions) % length)
    sines = np.where(pairs[:, None] == 0, np.cos(np.pi * positions)[None, :], np.sin(angle))
    return np.where(is_sin[:, None], sines, np.cos(angle))


def make_tables(groups_y, groups_x, rows, cols):
    length_x, length_y = groups_x * rows, groups_y * cols
    per = length_y // (groups_x * groups_y)
    half = per // 2
    ids = np.arange(length_y)
    pair_y = (ids // per) * half + ids % half
    sin_y = (ids % per) >= half
    forward_y = real_basis(pair_y, sin_y, np.arange(length_y), length_y)
    forward_y = forward_y.reshape(groups_y, cols, length_y)
    lanes = np.arange(cols + 128)
    local_y = np.where(lanes > cols, -1, lanes)
    keep_y = (lanes <= cols) | (lanes == cols + 127)
    inverse_y = np.stack(
        [
            real_basis(pair_y, sin_y, (h * cols + local_y) % length_y, length_y) * keep_y
            for h in range(groups_y)
        ]
    )
    kx = np.arange(length_x)
    pair_x = kx % (length_x // 2)
    sin_x = kx >= length_x // 2
    basis_x = real_basis(pair_x, sin_x, np.arange(length_x), length_x)
    forward_x = np.zeros((groups_x, 2, rows, 2, length_x))
    band = rows + 8
    inverse_x = np.zeros((2, length_x, groups_x, 128))
    local_x = np.arange(band)
    keep_x = (local_x <= rows) | (local_x == band - 1)
    local_x = np.where(local_x > rows, -1, local_x)
    for s in range(2):
        forward_x[:, s, :, s, :] = basis_x.T.reshape(groups_x, rows, length_x)
        for w in range(groups_x):
            part = basis_x[:, (w * rows + local_x) % length_x] * keep_x
            inverse_x[s, :, w, s * band : (s + 1) * band] = part
    forward_x = forward_x.reshape(groups_x, 2 * rows, 2 * length_x)
    inverse_x = inverse_x.reshape(2 * length_x, groups_x * 128)

    def halves(table, axis):
        coarse = table.astype(ml_dtypes.bfloat16)
        fine = (table - coarse.astype(np.float64)).astype(ml_dtypes.bfloat16)
        return np.stack([coarse, fine], axis=axis)

    forward_x = halves(forward_x, 1)
    forward_x = np.concatenate([forward_x[:, 0], forward_x[:, 0], forward_x[:, 1]], axis=1)
    return halves(forward_y, 1), halves(inverse_y, 1), forward_x, halves(inverse_x, 0)


def dot(a, b, dims=((1,), (0,))):
    return lax.dot_general(a, b, (dims, ((), ())), preferred_element_type=jnp.float32)


def put(ref, start, count, stride, value):
    for tile in range(ref.shape[0]):
        ref[tile, pl.ds(start, count, stride=stride), :] = value[:, tile * 128 : (tile + 1) * 128]


def take(ref, start, count, stride=1, tiles=None):
    rows = pl.ds(start, count, stride=stride)
    parts = [ref[tile, rows, :] for tile in range(tiles or ref.shape[0])]
    return jnp.concatenate(parts, axis=1)


def halved(value, axis):
    coarse = value.astype(jnp.bfloat16)
    fine = (value - coarse.astype(jnp.float32)).astype(jnp.bfloat16)
    return jnp.concatenate([coarse, fine], axis=axis)


def widened(lift, taps):
    empty = jnp.zeros((2, lift.shape[1]), jnp.float32)
    lift_wide, taps_wide = [], []
    for a in range(3):
        for k in range(2):
            lift_wide += [lift[k : k + 1]] * 3
            taps_wide += [taps[3 * a : 3 * a + 3]]
        lift_wide.append(empty)
        taps_wide.append(empty)
    return jnp.concatenate(lift_wide, axis=0), jnp.concatenate(taps_wide, axis=0)


def fused_kernel(
    groups_y,
    groups_x,
    rows,
    cols,
    vel_hbm,
    cot_hbm,
    lift_hbm,
    taps_hbm,
    point_hbm,
    outw_hbm,
    fy_hbm,
    iy_hbm,
    fx_hbm,
    ix_hbm,
    gv_hbm,
    sums_hbm,
    gv_ref,
    sums_ref,
    vel_ref,
    cot_ref,
    lift_ref,
    taps_ref,
    point_ref,
    outw_ref,
    fy,
    iy,
    fx,
    ix,
    gath,
    send2,
    recv2,
    send3,
    recv3,
    gath4,
    halo_out,
    halo_in,
    edge_out,
    edge_in,
    ext,
    shifts,
    tbuf,
    slope,
    gp2,
    ubuf,
    pay_y,
    pay_x,
    table_sem,
    s1,
    r1,
    s2,
    r2,
    s3,
    r3,
    s4,
    r4,
    sh,
    rh,
    se,
    re,
    s5,
    r5,
    s6,
    r6,
):
    bf16, f32 = jnp.bfloat16, jnp.float32
    h = lax.axis_index("ha")
    w = lax.axis_index("wa")
    length_x, length_y = groups_x * rows, groups_y * cols
    per = length_y // (groups_x * groups_y)
    half = per // 2
    wide = cols + 128
    band = rows + 8

    loads = [
        pltpu.make_async_copy(fy_hbm.at[h], fy, table_sem.at[0]),
        pltpu.make_async_copy(iy_hbm.at[h], iy, table_sem.at[1]),
        pltpu.make_async_copy(fx_hbm, fx, table_sem.at[2]),
        pltpu.make_async_copy(ix_hbm, ix, table_sem.at[3]),
    ]
    pairs = [
        (cot_hbm, cot_ref),
        (vel_hbm, vel_ref),
        (lift_hbm, lift_ref),
        (taps_hbm, taps_ref),
        (point_hbm, point_ref),
        (outw_hbm, outw_ref),
    ]
    small = [
        pltpu.make_async_copy(src, dst, table_sem.at[4 + i]) for i, (src, dst) in enumerate(pairs)
    ]
    for load in small + [loads[0], loads[2], loads[3], loads[1]]:
        load.start()

    def ha_peer(step):
        return lax.rem(h + step, groups_y)

    def wa_peer(step):
        return lax.rem(w + step, groups_x)

    barrier = pltpu.get_barrier_semaphore()
    for step in range(1, groups_y):
        pl.semaphore_signal(
            barrier, inc=1, device_id=(ha_peer(step), w), device_id_type=pl.DeviceIdType.MESH
        )
    for step in range(1, groups_x):
        pl.semaphore_signal(
            barrier, inc=1, device_id=(h, wa_peer(step)), device_id_type=pl.DeviceIdType.MESH
        )

    def remote(src, dst, send, recv, device):
        return pltpu.make_async_remote_copy(
            src_ref=src,
            dst_ref=dst,
            send_sem=send,
            recv_sem=recv,
            device_id=device,
            device_id_type=pl.DeviceIdType.MESH,
        )

    small[0].wait()
    gath[h] = halved(cot_ref[...].reshape(2 * rows, cols), 0)
    small[1].wait()
    vel = vel_ref[...].reshape(2 * rows, cols)
    halo_out[0] = vel[:, :128]
    halo_out[1] = vel[:, cols - 128 :]
    pl.semaphore_wait(barrier, groups_y + groups_x - 2)

    def spread_y(buf, send, recv):
        copies = []
        for step in range(1, groups_y):
            copy = remote(buf.at[h], buf.at[h], send.at[step], recv.at[h], (ha_peer(step), w))
            copy.start()
            copies.append(copy)
        return copies

    def arrived_y(buf, send, recv, step):
        src = ha_peer(step)
        remote(buf.at[src], buf.at[src], send.at[step], recv.at[src], (src, w)).wait_recv()
        return src

    def spread_x(src_of, buf, send, recv):
        copies = []
        for step in range(1, groups_x):
            dst = wa_peer(step)
            copy = remote(src_of(dst), buf.at[w], send.at[step], recv.at[w], (h, dst))
            copy.start()
            copies.append(copy)
        return copies

    def arrived_x(buf, send, recv, step):
        src = wa_peer(step)
        remote(buf.at[src], buf.at[src], send.at[step], recv.at[src], (h, src)).wait_recv()
        return src

    pending = spread_y(gath, s1, r1)
    left, right = (ha_peer(groups_y - 1), w), (ha_peer(1), w)
    halo = [
        remote(halo_out.at[0], halo_in.at[0], sh.at[0], rh.at[0], left),
        remote(halo_out.at[1], halo_in.at[1], sh.at[1], rh.at[1], right),
    ]
    for copy in halo:
        copy.start()

    for load in small[2:]:
        load.wait()
    lift = lift_ref[...]
    taps = taps_ref[:, 0, :]
    point = point_ref[0]
    outw = outw_ref[...].astype(f32)
    lift_wide, taps_wide = widened(lift, taps)
    both = lift_wide * taps_wide
    mixed = dot(halved(both, 0), point, ((1,), (1,)))
    mixed = mixed[:24] + mixed[24:]
    coarse = mixed.astype(bf16).astype(f32)
    stack = [coarse, mixed - coarse, coarse, jnp.zeros((56, 64), f32)]
    stack = jnp.pad(jnp.concatenate(stack, axis=0), ((0, 0), (0, 64)))
    mixed_b = jnp.transpose(stack)[:64, :80].astype(bf16)
    none = jnp.zeros((8, wide), f32)
    out_pad = jnp.concatenate([outw, jnp.zeros((14, 64), f32)], axis=0)
    columns = jnp.transpose(jnp.pad(out_pad, ((0, 112), (0, 64))))
    out_0 = jnp.broadcast_to(columns[:64, 0:1], (64, wide))
    out_1 = jnp.broadcast_to(columns[:64, 1:2], (64, wide))
    lift_pad = jnp.concatenate([lift, jnp.zeros((6, 64), f32)], axis=0)
    through = dot(halved(lift_pad, 0), out_pad.astype(bf16), ((1,), (1,)))
    through = through[:8] + through[8:]
    row_24 = lax.broadcasted_iota(jnp.int32, (24, 16), 0)
    place = jnp.where(row_24 == 9, through[0:1], jnp.where(row_24 == 12, through[1:2], 0.0))
    back_b = jnp.concatenate([mixed, place], axis=1).astype(bf16)

    row_id = lax.broadcasted_iota(jnp.int32, (per, length_x), 0)
    lane_id = lax.broadcasted_iota(jnp.int32, (per, length_x), 1)
    py = (h * groups_x + w) * half + lax.rem(row_id, half)
    px = lax.rem(lane_id, length_x // 2)
    ysin, xsin = row_id >= half, lane_id >= length_x // 2
    ky = jnp.where((py == 0) & ysin, length_y // 2, py).astype(f32)
    kx = jnp.where((px == 0) & xsin, length_x // 2, px).astype(f32)
    weight = jnp.where(py == 0, 1.0, 2.0) * jnp.where(px == 0, 1.0, 2.0) / (length_x * length_y)
    inverse_k = weight / jnp.maximum(kx * kx + ky * ky, 1.0)
    keep_0 = weight - kx * kx * inverse_k
    keep_1 = weight - ky * ky * inverse_k
    cross = kx * ky * inverse_k
    inner = (px != 0) & (py != 0)
    turn = jnp.where(inner, jnp.where(ysin == xsin, -cross, cross), 0.0)
    corner = jnp.where((px == 0) & (py == 0) & ysin & xsin, cross, 0.0)

    loads[0].wait()
    spec = jnp.zeros((cols, 2 * rows), f32)
    for step in range(groups_y):
        src = h if step == 0 else arrived_y(gath, s1, r1, step)
        where = pl.ds(pl.multiple_of(src * cols, cols), cols)
        field = gath[src]
        both_parts = dot(fy[0, :, where], field, ((1,), (1,)))
        spec = spec + both_parts[:, : 2 * rows] + both_parts[:, 2 * rows :]
        spec = spec + dot(fy[1, :, where], field[: 2 * rows], ((1,), (1,)))
    send2[...] = halved(spec, 1).reshape(groups_x, per, 4 * rows)
    pending += spread_x(lambda dst: send2.at[dst], recv2, s2, r2)
    recv2[w] = send2[w]

    for copy in halo:
        copy.wait()
    side = lax.broadcasted_iota(jnp.int32, (2 * rows, 128), 1)
    tail = jnp.where(side < 64, halo_in[0], halo_in[1])
    ext[:, :cols] = vel
    ext[:, cols:] = tail
    edge_out[...] = jnp.zeros_like(edge_out)
    for s in range(2):
        edge_out[0, 2 * s : 2 * s + 2, :] = ext[s * rows : s * rows + 2, :]
        edge_out[1, 2 * s : 2 * s + 2, :] = ext[s * rows + rows - 2 : s * rows + rows, :]
    edges = [
        remote(edge_out.at[0], edge_in.at[0], se.at[0], re.at[0], (h, wa_peer(groups_x - 1))),
        remote(edge_out.at[1], edge_in.at[1], se.at[1], re.at[1], (h, wa_peer(1))),
    ]
    for copy in edges:
        copy.start()
    shifts[...] = jnp.zeros_like(shifts)
    for s in range(2):
        for b in range(3):
            moved = ext[s * rows : (s + 1) * rows, :]
            if b != 1:
                moved = pltpu.roll(moved, (1 - b) % wide, 1)
            put(shifts, 16 + s * 3 + b, rows, 8, moved)

    def forward_row(n):
        start = n * 8 if isinstance(n, int) else pl.multiple_of(8 * n, 8)
        window = take(shifts, start, 24)
        coarse = window.astype(bf16).astype(f32)
        window = jnp.concatenate([coarse, coarse, window - coarse, none], axis=0)
        tan = jnp.tanh(dot(mixed_b, window.astype(bf16)))
        tbuf[n] = tan.astype(bf16)
        slope[n] = (1.0 - tan * tan).astype(bf16)

    def forward_rows(first, count):
        def two(i, carry):
            forward_row(first + 2 * i)
            forward_row(first + 2 * i + 1)
            return carry

        lax.fori_loop(0, count // 2, two, 0)

    forward_rows(2, 4)

    loads[2].wait()
    waves = jnp.zeros((per, 2 * length_x), f32)
    for step in range(groups_x):
        src = w if step == 0 else arrived_x(recv2, s2, r2, step)
        got = recv2[src]
        waves = waves + dot(jnp.concatenate([got, got[:, : 2 * rows]], axis=1), fx[src])
    a0, a1 = waves[:, :length_x], waves[:, length_x:]

    def swapped(a):
        a = jnp.concatenate([a[half:], a[:half]], axis=0)
        return jnp.concatenate([a[:, length_x // 2 :], a[:, : length_x // 2]], axis=1)

    p0 = keep_0 * a0 - turn * swapped(a1) - corner * a1
    p1 = keep_1 * a1 - turn * swapped(a0) - corner * a0
    loads[3].wait()
    split = halved(jnp.concatenate([p0, p1], axis=1), 0)
    fields = dot(split, ix[0])
    fields = fields[:per] + fields[per:] + dot(split[:per], ix[1])
    for dst in range(groups_x):
        send3[dst] = fields[:, dst * 128 : (dst + 1) * 128]
    pending += spread_x(lambda dst: send3.at[dst], recv3, s3, r3)
    recv3[w] = send3[w]

    forward_rows(6, 10)
    for copy in edges:
        copy.wait()
    for s in range(2):
        for b in range(3):
            for slot, first in ((1, 0), (0, rows + 2)):
                moved = edge_in[slot]
                if b != 1:
                    moved = pltpu.roll(moved, (1 - b) % wide, 1)
                for i in range(2):
                    at = 8 * (first + i) + s * 3 + b
                    put(shifts, at, 1, 1, moved[2 * s + i : 2 * s + i + 1])

    for step in range(1, groups_x):
        arrived_x(recv3, s3, r3, step)
    gath4[h] = halved(jnp.transpose(recv3[...].reshape(cols, 128))[: 2 * band], 0)
    pending += spread_y(gath4, s4, r4)

    forward_rows(16, rows - 16)
    for n in (0, 1, rows, rows + 1):
        forward_row(n)
    loads[1].wait()
    field = jnp.zeros((2 * band, wide), f32)
    for step in range(groups_y):
        src = h if step == 0 else arrived_y(gath4, s4, r4, step)
        where = pl.ds(pl.multiple_of(src * cols, cols), cols)
        got = gath4[src]
        both_parts = dot(got, iy[0, where, :])
        field = field + both_parts[: 2 * band] + both_parts[2 * band :]
        field = field + dot(got[: 2 * band], iy[1, where, :])
    gp2[...] = jnp.zeros_like(gp2)
    for s in range(2):
        part = field[s * band : (s + 1) * band]
        put(gp2, 8 + s, rows, 8, part[:rows])
        put(gp2, 8 * (rows + 1) + s, 1, 1, part[rows : rows + 1])
        put(gp2, s, 1, 1, part[band - 1 :])

    def backward_row(n, own):
        gp8 = take(gp2, pl.multiple_of(8 * n, 8), 8)
        gp16 = jnp.concatenate([gp8, jnp.zeros_like(gp8)], axis=0).astype(bf16)
        tan = tbuf[n]
        gpb = gp16.astype(f32)
        grad = out_0 * gpb[0:1] + out_1 * gpb[1:2]
        gz = (grad * slope[n].astype(f32)).astype(bf16)
        back = dot(back_b, jnp.concatenate([gz, gp16], axis=0))
        put(ubuf, pl.multiple_of(24 * n, 8), 24, 1, back)
        if not own:
            return None
        window = take(shifts, pl.multiple_of(8 * n, 8), 24, tiles=cols // 128)
        coarse = window.astype(bf16).astype(f32)
        pad = jnp.zeros_like(gp8[:, :cols])
        right_side = [window, gp8[:, :cols], window - coarse, pad]
        right_side = jnp.concatenate(right_side, axis=0).astype(bf16)
        left_side = jnp.concatenate([gz[:, :cols], tan[:, :cols], gp16[:, :cols]], axis=0)
        return dot(left_side, right_side, ((1,), (1,)))

    def backward_rows(i, total):
        for j in range(4):
            total = total + backward_row(1 + 4 * i + j, True)
        return total

    acc = lax.fori_loop(0, rows // 4, backward_rows, jnp.zeros((144, 64), f32))
    acc = acc[:, :32] + acc[:, 32:]

    low = lax.broadcasted_iota(jnp.int32, (64, 32), 1) < 24
    packed = jnp.concatenate(
        [jnp.where(low, acc[:64], acc[64:128]), acc[128:144], jnp.zeros((48, 32), f32)], axis=0
    )
    packed = jnp.transpose(jnp.pad(packed, ((0, 0), (0, 96))))[:32]
    upper = [packed[16:26, :64], packed[9:10, 64:], packed[12:13, 64:], packed[28:32, :64]]
    upper = jnp.concatenate(upper, axis=0)
    pay_y[h] = jnp.concatenate([packed[:16, :64], upper], axis=1)
    pending += spread_y(pay_y, s5, r5)

    backward_row(0, False)
    backward_row(rows + 1, False)
    for s in range(2):
        result = take(gp2, 8 + s, rows, 8)
        for b in range(3):
            k = s * 3 + b
            part = (
                take(ubuf, 48 + k, rows, 24)
                + take(ubuf, 24 + 8 + k, rows, 24)
                + take(ubuf, 16 + k, rows, 24)
            )
            if b != 1:
                part = pltpu.roll(part, (b - 1) % wide, 1)
            result = result + part
        gv_ref[s] = result[:, :cols]
    leave_gv = pltpu.make_async_copy(gv_ref, gv_hbm, table_sem.at[10])
    leave_gv.start()

    for step in range(1, groups_y):
        arrived_y(pay_y, s5, r5, step)
    summed = pay_y[0]
    for src in range(1, groups_y):
        summed = summed + pay_y[src]
    pay_x[w] = summed
    pending += spread_x(lambda dst: pay_x.at[w], pay_x, s6, r6)
    for step in range(1, groups_x):
        arrived_x(pay_x, s6, r6, step)
    sums = pay_x[0]
    for src in range(1, groups_x):
        sums = sums + pay_x[src]
    sums = sums * (1.0 / math.sqrt(length_x * length_y))
    sums_ref[...] = sums
    leave = pltpu.make_async_copy(sums_ref, sums_hbm, table_sem.at[11])
    leave.start()
    for copy in pending:
        copy.wait_send()
    leave_gv.wait()
    leave.wait()


def finish_kernel(
    gv_in,
    sums_hbm,
    lift_hbm,
    taps_hbm,
    point_hbm,
    outw_hbm,
    gv_out,
    lift_out,
    taps_out,
    point_out,
    out_out,
    sums_ref,
    lift_ref,
    taps_ref,
    point_ref,
    outw_ref,
    glift_ref,
    gtaps_ref,
    gpoint_ref,
    gout_ref,
    sem,
):
    bf16, f32 = jnp.bfloat16, jnp.float32
    pairs = [
        (sums_hbm, sums_ref),
        (lift_hbm, lift_ref),
        (taps_hbm, taps_ref),
        (point_hbm, point_ref),
        (outw_hbm, outw_ref),
    ]
    loads = [pltpu.make_async_copy(a, b, sem.at[i]) for i, (a, b) in enumerate(pairs)]
    pairs = [
        (gv_in, gv_out),
        (glift_ref, lift_out),
        (gtaps_ref, taps_out),
        (gpoint_ref, point_out),
        (gout_ref, out_out),
    ]
    stores = [pltpu.make_async_copy(a, b, sem.at[5 + i]) for i, (a, b) in enumerate(pairs)]
    for load in loads:
        load.start()
    stores[0].start()
    for load in loads:
        load.wait()
    sums = sums_ref[...]
    lift = lift_ref[...]
    point = point_ref[0]
    outw = outw_ref[...].astype(f32)
    lift_wide, taps_wide = widened(lift, taps_ref[:, 0, :])
    both = lift_wide * taps_wide
    gz_sum = jnp.concatenate([sums[:, :64], sums[:8, 64:]], axis=0)
    depth = dot(halved(gz_sum, 0), point)
    depth = depth[:24] + depth[24:]
    fine = gz_sum - gz_sum.astype(bf16).astype(f32)
    left_side = jnp.concatenate([gz_sum, fine, gz_sum, jnp.zeros((56, 64), f32)], axis=0)
    left_side = jnp.transpose(jnp.pad(left_side, ((0, 0), (0, 64))))[:64, :80].astype(bf16)
    fine = both - both.astype(bf16).astype(f32)
    right_side = jnp.concatenate([both, both, fine, jnp.zeros((8, 64), f32)], axis=0).astype(bf16)
    gpoint_ref[0] = dot(left_side, right_side)
    by_tap = depth * lift_wide
    by_lift = depth * taps_wide
    for a in range(3):
        for b in range(3):
            k = 8 * a + b
            gtaps_ref[3 * a + b] = by_tap[k : k + 1] + by_tap[k + 3 : k + 4]
    for s in range(2):
        total = jnp.zeros((1, 64), f32)
        for a in range(3):
            k = 8 * a + 3 * s
            total = total + jnp.sum(by_lift[k : k + 3], axis=0, keepdims=True)
        for r in range(2):
            total = total + sums[10 + s : 11 + s, 64 + r : 65 + r] * outw[r : r + 1]
        glift_ref[s : s + 1] = total
        total = sums[8 + s : 9 + s, 64:]
        for r in range(2):
            total = total + sums[10 + r : 11 + r, 64 + s : 65 + s] * lift[r : r + 1]
        gout_ref[s : s + 1] = total
    for store in stores[1:]:
        store.start()
    for store in stores:
        store.wait()


def fused(velocity, cotangent, lift_weight, depth_kernels, point_weights, out_weight):
    groups_y, groups_x = lax.axis_size("ha"), lax.axis_size("wa")
    _, rows, cols = velocity.shape
    channels = lift_weight.shape[0]
    length_x, length_y = groups_x * rows, groups_y * cols
    per = length_y // (groups_x * groups_y)
    wide = cols + 128
    tables = make_tables(groups_y, groups_x, rows, cols)
    bf16, f32 = jnp.bfloat16, jnp.float32
    dma = pltpu.SemaphoreType.DMA
    hbm = pl.BlockSpec(memory_space=pltpu.HBM)
    lift_t = lift_weight.T
    taps_t = jnp.transpose(depth_kernels, (2, 0, 1))
    grad_velocity, sums = pl.pallas_call(
        functools.partial(fused_kernel, groups_y, groups_x, rows, cols),
        out_shape=(
            jax.ShapeDtypeStruct((2, rows, cols), f32),
            jax.ShapeDtypeStruct((16, 128), f32),
        ),
        in_specs=[hbm] * 10,
        out_specs=(hbm, hbm),
        scratch_shapes=[
            pltpu.VMEM((2, rows, cols), f32),
            pltpu.VMEM((16, 128), f32),
            pltpu.VMEM((2, rows, cols), f32),
            pltpu.VMEM((2, rows, cols), f32),
            pltpu.VMEM((2, channels), f32),
            pltpu.VMEM((9, 1, channels), f32),
            pltpu.VMEM((1, channels, channels), bf16),
            pltpu.VMEM((2, channels), bf16),
            pltpu.VMEM((2, cols, length_y), bf16),
            pltpu.VMEM((2, length_y, wide), bf16),
            pltpu.VMEM((groups_x, 6 * rows, 2 * length_x), bf16),
            pltpu.VMEM((2, 2 * length_x, groups_x * 128), bf16),
            pltpu.VMEM((groups_y, 4 * rows, cols), bf16),
            pltpu.VMEM((groups_x, per, 4 * rows), bf16),
            pltpu.VMEM((groups_x, per, 4 * rows), bf16),
            pltpu.VMEM((groups_x, per, 128), f32),
            pltpu.VMEM((groups_x, per, 128), f32),
            pltpu.VMEM((groups_y, 4 * (rows + 8), cols), bf16),
            pltpu.VMEM((2, 2 * rows, 128), f32),
            pltpu.VMEM((2, 2 * rows, 128), f32),
            pltpu.VMEM((2, 8, wide), f32),
            pltpu.VMEM((2, 8, wide), f32),
            pltpu.VMEM((2 * rows, wide), f32),
            pltpu.VMEM((wide // 128, 8 * (rows + 4), 128), f32),
            pltpu.VMEM((rows + 2, channels, wide), bf16),
            pltpu.VMEM((rows + 2, channels, wide), bf16),
            pltpu.VMEM((wide // 128, 8 * (rows + 2), 128), f32),
            pltpu.VMEM((wide // 128, 24 * (rows + 2), 128), f32),
            pltpu.VMEM((groups_y, 16, 128), f32),
            pltpu.VMEM((groups_x, 16, 128), f32),
            dma((12,)),
            dma((groups_y,)),
            dma((groups_y,)),
            dma((groups_x,)),
            dma((groups_x,)),
            dma((groups_x,)),
            dma((groups_x,)),
            dma((groups_y,)),
            dma((groups_y,)),
            dma((2,)),
            dma((2,)),
            dma((2,)),
            dma((2,)),
            dma((groups_y,)),
            dma((groups_y,)),
            dma((groups_x,)),
            dma((groups_x,)),
        ],
        compiler_params=pltpu.CompilerParams(
            collective_id=0, has_side_effects=True, vmem_limit_bytes=64 * 1024 * 1024
        ),
    )(
        velocity,
        cotangent,
        lift_t,
        taps_t,
        point_weights,
        out_weight,
        *[jnp.asarray(t) for t in tables],
    )
    results = pl.pallas_call(
        finish_kernel,
        out_shape=(
            jax.ShapeDtypeStruct((2, rows, cols), f32),
            jax.ShapeDtypeStruct((2, channels), f32),
            jax.ShapeDtypeStruct((9, 1, channels), f32),
            jax.ShapeDtypeStruct((1, channels, channels), f32),
            jax.ShapeDtypeStruct((2, channels), f32),
        ),
        in_specs=[hbm] * 6,
        out_specs=(hbm,) * 5,
        scratch_shapes=[
            pltpu.VMEM((16, 128), f32),
            pltpu.VMEM((2, channels), f32),
            pltpu.VMEM((9, 1, channels), f32),
            pltpu.VMEM((1, channels, channels), bf16),
            pltpu.VMEM((2, channels), bf16),
            pltpu.VMEM((2, channels), f32),
            pltpu.VMEM((9, 1, channels), f32),
            pltpu.VMEM((1, channels, channels), f32),
            pltpu.VMEM((2, channels), f32),
            dma((10,)),
        ],
        compiler_params=pltpu.CompilerParams(vmem_limit_bytes=64 * 1024 * 1024),
    )(grad_velocity, sums, lift_t, taps_t, point_weights, out_weight)
    grad_velocity, grad_lift, grad_taps, grad_point, grad_out = results
    return grad_velocity, grad_lift.T, jnp.transpose(grad_taps, (1, 2, 0)), grad_point, grad_out


def either(velocity, cotangent, lift_weight, depth_kernels, point_weights, out_weight):
    groups_y, groups_x = lax.axis_size("ha"), lax.axis_size("wa")
    layers, channels, _ = depth_kernels.shape
    _, rows, cols = velocity.shape
    per = groups_y * cols // (groups_x * groups_y)
    fits = layers == 1 and channels == 64 and rows == 32 and cols % 256 == 0
    fits = fits and per % 32 == 0 and groups_y * cols <= 1024 and groups_x * rows == 256
    run = fused if fits else local
    return run(velocity, cotangent, lift_weight, depth_kernels, point_weights, out_weight)


def solution(mesh):
    return jax.shard_map(
        either,
        mesh=mesh,
        in_specs=(P(None, "wa", "ha"), P(None, "wa", "ha"), P(), P(), P(), P()),
        out_specs=(P(None, "wa", "ha"), P(), P(), P(), P()),
        check_vma=False,
    )
```
